128 devices in a mesh: tile: 16 (over x_lo, y, core), frame: 8 (over z, x_hi).
Axes of the slice: x: 4 (x_hi: 2, x_lo: 2; x = x_hi * 2 + x_lo), y: 4, z: 4, core: 2. Of those that a mesh axis runs over, the one named last changes fastest.
Arguments:
- tokens: bfloat16 [16, 24, 128, 768], P('frame', None, 'tile'), may hold values from -6 to 6
- gain_space: float32 [768], replicated, may hold values from 0.5 to 1.5
- qkv_space: bfloat16 [768, 2304], replicated, may hold values from -2 to 2
- out_space: bfloat16 [768, 768], replicated, may hold values from -0.21875 to 0.21875
- gain_time: float32 [768], replicated, may hold values from 0.5 to 1.5
- qkv_time: bfloat16 [768, 2304], replicated, may hold values from -2 to 2
- out_time: bfloat16 [768, 768], replicated, may hold values from -0.21875 to 0.21875
- cotangent: bfloat16 [16, 24, 128, 768], P('frame', None, 'tile'), may hold values from -6 to 6
Outputs:
- layer_out: bfloat16 [16, 24, 128, 768], P('frame', None, 'tile')
- grad_tokens: float32 [16, 24, 128, 768], P('frame', None, 'tile')
- grad_gain_space: float32 [768], P(('tile', 'frame'))
- grad_qkv_space: float32 [768, 2304], P(('tile', 'frame'))
- grad_out_space: float32 [768, 768], P(('tile', 'frame'))
- grad_gain_time: float32 [768], P(('tile', 'frame'))
- grad_qkv_time: float32 [768, 2304], P(('tile', 'frame'))
- grad_out_time: float32 [768, 768], P(('tile', 'frame'))
The draws below stay inside these ranges and needn't reach their ends.
All inputs are finite; a program needn't handle non-finite values.
Results may differ from the reference program's by a relative error of at most 0.025.
Values may be sent and summed in bfloat16 or wider, within the bound.
No kernel may reach another device: no remote copies, remote signals or barrier semaphores. Data moves between devices by JAX's collectives and lax.ppermute only.
A program may use at most 192 MiB of HBM per device.

```python
import math
import jax
import jax.numpy as jnp
from jax import lax

HEADS = 12
HDIM = 64
D = 768
BH = 8
LAT = 24
TW = 8
F = 16
LON = 128
TOKENS = 49152


def packed_projection(key, salt_value):
    base_key = jax.random.fold_in(key, salt_value)
    key_query, key_key, key_value = jax.random.split(base_key, 3)
    features = HEADS * HDIM
    fan_scale = features ** (-0.5)
    query_map = jax.random.normal(key_query, (features, features), jnp.float32) * fan_scale
    key_map = jax.random.normal(key_key, (features, features), jnp.float32) * fan_scale
    value_map = jax.random.normal(key_value, (features, features), jnp.float32) * fan_scale
    packed = jnp.concatenate([query_map, key_map, value_map], axis=1)
    return jnp.clip(packed, -2.0, 2.0).astype(jnp.bfloat16)


def draw_qkv_space(key, part):
    return packed_projection(key, 11)


def draw_qkv_time(key, part):
    return packed_projection(key, 23)


def with_spikes(values, rng, source, target, shards_of, factor):
    owner, partner = [(jnp.arange(values.shape[dim]) // (values.shape[dim] // shards_of)).reshape([-1 if axis == dim else 1 for axis in range(values.ndim)]) for dim in (source, target)]
    chosen = jax.random.permutation(rng, shards_of)[partner]
    strong = (owner == chosen) | (owner == (partner + shards_of // 2) % shards_of)
    return jnp.where(strong, factor * values, values)


def level_of(stream_key, extent, shards, low, top_value):
    loudness, own = 1.0, jax.random.fold_in(stream_key, 6)
    for position, blocks in shards:
        steps = jnp.exp(jax.random.uniform(jax.random.fold_in(own, position), (blocks,), jnp.float32, low / len(shards), top_value / len(shards)))
        loudness = loudness * jnp.repeat(steps, extent[position] // blocks).reshape([-1 if axis == position else 1 for axis in range(len(extent))])
    return loudness


def normal_values(rng, extent, scale, limit, cuts=(), kind=jnp.bfloat16):
    factor_of = level_of(rng, extent, cuts, -0.22, 0.18) if cuts else 1.0
    drawn = jax.random.normal(rng, extent, jnp.float32) * scale * factor_of
    return jnp.minimum(jnp.maximum(drawn, -limit), limit).astype(kind)


def gaussian_with(key, dims, spread, limit, cuts, heavy, kind=jnp.bfloat16):
    values = spread * jax.random.normal(key, dims, jnp.float32)
    if cuts:
        values = values * level_of(key, dims, cuts, -0.22, 0.18)
    return jnp.clip(with_spikes(values, jax.random.fold_in(key, 3), *heavy), -limit, limit).astype(kind)


def setup_inputs(seed: int = 0) -> dict:
    streams_of = jax.random.split(jax.random.key(seed), 9)
    tokens = gaussian_with(streams_of[0], (F, LAT, LON, D), 1.0, 6.0, ((0, 8), (2, 16)), (2, 3, 16, 2.0))
    gain_space = jnp.clip(1.0 + 0.1 * jax.random.normal(streams_of[1], (D,), jnp.float32), 0.5, 1.5)
    qkv_space = draw_qkv_space(jax.random.fold_in(streams_of[8], 71), 0)
    out_space = normal_values(streams_of[3], (D, D), D ** -0.5, 0.21875)
    gain_time = jnp.clip(1.0 + 0.1 * jax.random.normal(streams_of[4], (D,), jnp.float32), 0.5, 1.5)
    qkv_time = draw_qkv_time(jax.random.fold_in(streams_of[8], 71), 0)
    out_time = normal_values(streams_of[6], (D, D), D ** -0.5, 0.21875)
    cotangent = gaussian_with(streams_of[7], (F, LAT, LON, D), 1.0, 6.0, ((0, 8), (2, 16)), (2, 3, 16, 2.0))
    return {"tokens": tokens, "gain_space": gain_space, "qkv_space": qkv_space, "out_space": out_space, "gain_time": gain_time, "qkv_time": qkv_time, "out_time": out_time, "cotangent": cotangent}


norm_eps = 1e-05

def layer_norm(row_vals, gain_vec):
    centre_mean = lax.optimization_barrier(jnp.mean(row_vals, axis=-1, keepdims=True))
    centred = row_vals - centre_mean
    variance = lax.optimization_barrier(jnp.mean(centred * centred, axis=-1, keepdims=True))
    return (centred * lax.rsqrt(variance + norm_eps) * gain_vec).astype(jnp.bfloat16)

def project(in_rows, weight):
    flat_rows = in_rows.reshape(-1, in_rows.shape[-1])
    result = jnp.dot(flat_rows, weight, preferred_element_type=jnp.float32)
    return result.astype(jnp.bfloat16).reshape(in_rows.shape[:-1] + (weight.shape[1],))

def residual_term(in_rows, weight):
    flat_rows = in_rows.reshape(-1, in_rows.shape[-1])
    result = jnp.dot(flat_rows, weight, preferred_element_type=jnp.float32)
    return result.reshape(in_rows.shape[:-1] + (weight.shape[1],))

def back_project(cot_rows, weight):
    flat_rows = cot_rows.reshape(-1, cot_rows.shape[-1])
    result = lax.dot_general(flat_rows, weight, (((1,), (1,)), ((), ())), preferred_element_type=jnp.float32)
    return result.astype(jnp.bfloat16).reshape(cot_rows.shape[:-1] + (weight.shape[0],))

def weight_term(left_rows, right_rows):
    left_flat = left_rows.reshape(-1, left_rows.shape[-1])
    right_flat = right_rows.reshape(-1, right_rows.shape[-1])
    return lax.dot_general(left_flat, right_flat, (((0,), (0,)), ((), ())), preferred_element_type=jnp.float32)

def spatial_core(queries, keyval):
    lat_rows, tile_width, features = queries.shape
    head_count = features // HDIM
    blocks = lat_rows // BH
    query_blocks = queries.astype(jnp.float32).reshape(blocks, BH * tile_width, head_count, HDIM)
    pole_pad = jnp.zeros((BH, 3 * tile_width, 2 * features), keyval.dtype)
    padded = jnp.concatenate([pole_pad, keyval, pole_pad], axis=0).astype(jnp.float32)
    padded = padded.reshape(blocks + 2, BH, 3 * tile_width, 2 * features)
    stacked = jnp.concatenate([padded[:-2], padded[1:-1], padded[2:]], axis=1)
    stacked = stacked.reshape(blocks, 9 * BH * tile_width, 2, head_count, HDIM)
    scores = jnp.einsum('bqhd,bkhd->bhqk', query_blocks, stacked[:, :, 0]) * HDIM ** (-0.5)
    block_index = jnp.arange(blocks)[:, None] + jnp.arange(3)[None, :] - 1
    valid_keys = jnp.repeat((block_index >= 0) & (block_index < blocks), 3 * BH * tile_width, axis=1)
    scores = jnp.where(valid_keys[:, None, None, :], scores, -1e+30)
    row_max = lax.optimization_barrier(jnp.max(scores, axis=-1, keepdims=True))
    exponent = jnp.exp(scores - row_max)
    weights = (exponent / lax.optimization_barrier(jnp.sum(exponent, axis=-1, keepdims=True))).astype(jnp.bfloat16)
    mixed_rows = jnp.einsum('bhqk,bkhd->bqhd', weights.astype(jnp.float32), stacked[:, :, 1])
    return mixed_rows.reshape(lat_rows, tile_width, features).astype(jnp.bfloat16)

def temporal_core(packed):
    frame_count, count_tokens, triple_width = packed.shape
    features = triple_width // 3
    head_count = features // HDIM
    sections = packed.astype(jnp.float32).reshape(frame_count, count_tokens, 3, head_count, HDIM)
    scores = jnp.einsum('fnhd,gnhd->nhfg', sections[:, :, 0], sections[:, :, 1]) * HDIM ** (-0.5)
    row_max = lax.optimization_barrier(jnp.max(scores, axis=-1, keepdims=True))
    exponent = jnp.exp(scores - row_max)
    weights = (exponent / lax.optimization_barrier(jnp.sum(exponent, axis=-1, keepdims=True))).astype(jnp.bfloat16)
    mixed_rows = jnp.einsum('nhfg,gnhd->fnhd', weights.astype(jnp.float32), sections[:, :, 2])
    return mixed_rows.reshape(frame_count, count_tokens, features).astype(jnp.bfloat16)

def arrange(queries, keyval, tile_count):
    lat_rows, lon_cols, features = queries.shape
    tiled_query = queries.reshape(lat_rows, tile_count, TW, features).transpose(1, 0, 2, 3)
    tiled_keyval = keyval.reshape(lat_rows, tile_count, TW, 2 * features).transpose(1, 0, 2, 3)
    extended = jnp.concatenate([jnp.roll(tiled_keyval, 1, axis=0), tiled_keyval, jnp.roll(tiled_keyval, -1, axis=0)], axis=2)
    return (tiled_query, extended)

def reference(tokens, gain_space, qkv_space, out_space, gain_time, qkv_time, out_time, cotangent):
    frame_count, lat_rows, lon_cols, features = tokens.shape
    tile_count = lon_cols // TW
    tokens_wide = tokens.astype(jnp.float32)
    y_space, norm_back_space = jax.vjp(layer_norm, tokens_wide, gain_space)
    packed_space = project(y_space, qkv_space)
    query_space = packed_space[..., :features]
    keyval_space = packed_space[..., features:]

    def frame_forward(couple):
        tiled_query, extended = arrange(couple[0], couple[1], tile_count)
        tiled_out = lax.map(lambda member: spatial_core(member[0], member[1]), (tiled_query, extended))
        return tiled_out.transpose(1, 0, 2, 3).reshape(lat_rows, lon_cols, features)
    o_space = lax.map(frame_forward, (query_space, keyval_space))
    x_mid = (tokens_wide + residual_term(o_space, out_space)).astype(jnp.bfloat16)
    y_time, norm_back_time = jax.vjp(layer_norm, x_mid.astype(jnp.float32), gain_time)
    packed_time = project(y_time, qkv_time)
    packed_rows = packed_time.transpose(1, 0, 2, 3)
    o_time = lax.map(temporal_core, packed_rows).transpose(1, 0, 2, 3)
    layer_out = (x_mid.astype(jnp.float32) + residual_term(o_time, out_time)).astype(jnp.bfloat16)
    d_proj_time = back_project(cotangent, out_time)

    def time_back(couple):
        return jax.vjp(temporal_core, couple[0])[1](couple[1])[0]
    d_packed_time = lax.map(time_back, (packed_rows, d_proj_time.transpose(1, 0, 2, 3))).transpose(1, 0, 2, 3)
    d_y_time = back_project(d_packed_time, qkv_time)
    d_norm_mid, d_gain_time = norm_back_time(d_y_time)
    d_mid = cotangent.astype(jnp.float32) + d_norm_mid
    d_mid_b = d_mid.astype(jnp.bfloat16)
    d_proj_space = back_project(d_mid_b, out_space)

    def frame_back(triple):
        tiled_query, extended = arrange(triple[0], triple[1], tile_count)
        tiled_grad = triple[2].reshape(lat_rows, tile_count, TW, features).transpose(1, 0, 2, 3)

        def member_back(member):
            return jax.vjp(spatial_core, member[0], member[1])[1](member[2])
        d_query, d_extended = lax.map(member_back, (tiled_query, extended, tiled_grad))
        d_keyval = d_extended[:, :, TW:2 * TW] + jnp.roll(d_extended[:, :, :TW], -1, axis=0) + jnp.roll(d_extended[:, :, 2 * TW:], 1, axis=0)
        d_query = d_query.transpose(1, 0, 2, 3).reshape(lat_rows, lon_cols, features)
        d_keyval = d_keyval.transpose(1, 0, 2, 3).reshape(lat_rows, lon_cols, 2 * features)
        return jnp.concatenate([d_query, d_keyval], axis=-1)
    d_packed_space = lax.map(frame_back, (query_space, keyval_space, d_proj_space))
    d_y_space = back_project(d_packed_space, qkv_space)
    d_norm_tokens, d_gain_space = norm_back_space(d_y_space)
    grad_tokens = d_mid + d_norm_tokens
    grad_scale = 1.0 / math.sqrt(TOKENS)
    return (layer_out, grad_tokens, d_gain_space * grad_scale, weight_term(y_space, d_packed_space) * grad_scale, weight_term(o_space, d_mid_b) * grad_scale, d_gain_time * grad_scale, weight_term(y_time, d_packed_time) * grad_scale, weight_term(o_time, cotangent) * grad_scale)
```

```python
import functools
import math

import jax
import jax.numpy as jnp
from jax import lax
from jax.experimental import pallas as pl
from jax.experimental.pallas import tpu as pltpu
from jax.sharding import Mesh
from jax.sharding import PartitionSpec as P

HDIM = 64
BH = 8
LANES = 4 * HDIM
EPS = 1e-05
F32 = jnp.float32
BF16 = jnp.bfloat16
TILE = ("xlo", "y", "core")
FRAME = ("z", "xhi")
VMEM_LIMIT = 56 * 1024 * 1024


def dot(left, right, left_dim=1, right_dim=0):
    return lax.dot_general(
        left, right, (((left_dim,), (right_dim,)), ((), ())), preferred_element_type=F32
    )


def normalized(rows):
    centred = rows - jnp.mean(rows, axis=-1, keepdims=True)
    variance = jnp.mean(centred * centred, axis=-1, keepdims=True)
    inverse = lax.rsqrt(variance + EPS)
    return centred * inverse, inverse


def norm_back(unit, inverse, gain, d_out):
    d_unit = d_out * gain
    along = jnp.mean(d_unit * unit, axis=-1, keepdims=True)
    return inverse * (d_unit - jnp.mean(d_unit, axis=-1, keepdims=True) - unit * along)


def head_mask(rows):
    row_head = lax.broadcasted_iota(jnp.int32, (4 * rows, LANES), 0) // rows
    lane_head = lax.broadcasted_iota(jnp.int32, (4 * rows, LANES), 1) // HDIM
    return row_head == lane_head


def spread(group, mask):
    stacked = jnp.concatenate([group] * 4, axis=0)
    return jnp.where(mask, stacked, jnp.zeros_like(stacked))


def gathered(wide, rows):
    lane_head = lax.broadcasted_iota(jnp.int32, (rows, LANES), 1) // HDIM
    parts = [wide[h * rows : (h + 1) * rows] for h in range(4)]
    low = jnp.where(lane_head == 0, parts[0], parts[1])
    high = jnp.where(lane_head == 2, parts[2], parts[3])
    return jnp.where(lane_head < 2, low, high)


def softmax_rows(scores):
    top = jnp.max(scores, axis=0, keepdims=True)
    exponent = jnp.exp(scores - top)
    return exponent * (1.0 / jnp.sum(exponent, axis=0, keepdims=True))


def key_ranges(blocks, step):
    return [(max(b - 1, 0) * step, min(b + 2, blocks) * step) for b in range(blocks)]


def spatial_forward_kernel(
    own_ref, west_ref, east_ref, gain_ref, qkv_ref, out_ref,
    y_ref, q_ref, kv_ref, p_ref, o_ref, mid_ref,
):
    _, lat, width, features = own_ref.shape
    rows = BH * width
    blocks = lat // BH
    step = 3 * rows
    gain = gain_ref[...]
    for tile, ref in enumerate((west_ref, own_ref, east_ref)):
        wide = ref[0].astype(F32).reshape(lat * width, features)
        unit, _ = normalized(wide)
        y = (unit * gain).astype(BF16)
        for b in range(blocks):
            at = b * step + tile * rows
            y_ref[0, at : at + rows] = y[b * rows : (b + 1) * rows]
        if tile == 1:
            q_ref[0] = (dot(y, qkv_ref[:, :features]).astype(BF16) * HDIM ** (-0.5)).astype(BF16)
    for b in range(blocks):
        part = slice(b * step, (b + 1) * step)
        kv_ref[0, part] = dot(y_ref[0, part], qkv_ref[:, features:]).astype(BF16)
    mask = head_mask(rows)
    offset = 0
    for b, (low, high) in enumerate(key_ranges(blocks, step)):
        span = high - low
        for g in range(features // LANES):
            lanes = slice(g * LANES, (g + 1) * LANES)
            queries = spread(q_ref[0, b * rows : (b + 1) * rows, lanes], mask)
            keys = kv_ref[0, low:high, lanes]
            values = kv_ref[0, low:high, features + g * LANES : features + (g + 1) * LANES]
            weights = softmax_rows(dot(keys, queries, 1, 1)).astype(BF16)
            p_ref[0, g, offset : offset + span] = weights
            mixed = dot(weights, values, 0, 0)
            o_ref[0, b * rows : (b + 1) * rows, lanes] = gathered(mixed, rows).astype(BF16)
        offset += span
    wide = own_ref[0].astype(F32).reshape(lat * width, features)
    mid = wide + dot(o_ref[0], out_ref[...])
    mid_ref[0] = mid.reshape(lat, width, features).astype(BF16)


def full(shape):
    return pl.BlockSpec(shape, lambda *_: (0,) * len(shape))


def per_step(shape):
    return pl.BlockSpec((1,) + shape, lambda i: (i,) + (0,) * len(shape))


def spatial_forward(own, west, east, gain, qkv, out):
    frames, lat, width, features = own.shape
    rows = lat * width
    blocks = lat // BH
    spans = sum(h - l for l, h in key_ranges(blocks, 3 * BH * width))
    groups = features // LANES
    outs = (
        ((3 * rows, features), BF16),
        ((rows, features), BF16),
        ((3 * rows, 2 * features), BF16),
        ((groups, spans, LANES), BF16),
        ((rows, features), BF16),
        ((lat, width, features), BF16),
    )
    return pl.pallas_call(
        spatial_forward_kernel,
        grid=(frames,),
        in_specs=[per_step((lat, width, features))] * 3
        + [full((1, features)), full(qkv.shape), full(out.shape)],
        out_specs=[per_step(shape) for shape, _ in outs],
        out_shape=[jax.ShapeDtypeStruct((frames,) + shape, kind) for shape, kind in outs],
        compiler_params=pltpu.CompilerParams(vmem_limit_bytes=VMEM_LIMIT),
        name="spatial_forward",
    )(own, west, east, gain, qkv, out)


def temporal_kernel(
    mid_ref, cot_ref, gain_ref, qkv_ref, out_ref,
    layer_ref, dmid_ref, y_ref, dpacked_ref, o_ref,
    packed_ref, dproj_ref,
):
    frames, _, width, features = mid_ref.shape
    rows = frames * width
    gain = gain_ref[...]
    mid = mid_ref[:, 0].astype(F32).reshape(rows, features)
    cot = cot_ref[:, 0].astype(F32).reshape(rows, features)
    unit, inverse = normalized(mid)
    y = (unit * gain).astype(BF16)
    y_ref[...] = y
    packed_ref[...] = dot(y, qkv_ref[...]).astype(BF16)
    dproj_ref[...] = dot(cot.astype(BF16), out_ref[...], 1, 1).astype(BF16)
    mask = head_mask(rows)
    key_col = lax.broadcasted_iota(jnp.int32, (rows, 4 * rows), 0) % width
    query_col = lax.broadcasted_iota(jnp.int32, (rows, 4 * rows), 1) % width
    same = key_col == query_col
    scale = HDIM ** (-0.5)
    for g in range(features // LANES):
        lanes = [slice(s * features + g * LANES, s * features + (g + 1) * LANES) for s in range(3)]
        queries = spread((packed_ref[:, lanes[0]] * scale).astype(BF16), mask)
        keys = packed_ref[:, lanes[1]]
        values = packed_ref[:, lanes[2]]
        scores = jnp.where(same, dot(keys, queries, 1, 1), -1e30)
        wide = softmax_rows(scores)
        weights = wide.astype(BF16)
        mixed = dot(weights, values, 0, 0)
        o_ref[:, lanes[0]] = gathered(mixed, rows).astype(BF16)
        d_out = spread(dproj_ref[:, lanes[0]], mask)
        d_weights = dot(values, d_out, 1, 1)
        delta = jnp.sum(wide * d_weights, axis=0, keepdims=True)
        d_scores = (wide * (d_weights - delta)).astype(BF16)
        d_query = gathered(dot(d_scores, keys, 0, 0), rows) * scale
        dpacked_ref[:, lanes[0]] = d_query.astype(BF16)
        dpacked_ref[:, lanes[1]] = dot(d_scores, queries).astype(BF16)
        dpacked_ref[:, lanes[2]] = dot(weights, d_out).astype(BF16)
    layer = mid + dot(o_ref[...], out_ref[...])
    layer_ref[:, 0] = layer.reshape(frames, width, features).astype(BF16)
    d_y = dot(dpacked_ref[...], qkv_ref[...], 1, 1)
    d_mid = cot + norm_back(unit, inverse, gain, d_y)
    dmid_ref[:, 0] = d_mid.reshape(frames, width, features).astype(BF16)


def temporal(mid, cot, gain, qkv, out):
    frames, lat, width, features = mid.shape
    rows = frames * width
    moved = pl.BlockSpec((frames, 1, width, features), lambda i: (0, i, 0, 0))

    def flat(columns):
        return pl.BlockSpec((rows, columns), lambda i: (i, 0))

    return pl.pallas_call(
        temporal_kernel,
        grid=(lat,),
        in_specs=[moved, moved, full((1, features)), full(qkv.shape), full(out.shape)],
        out_specs=[moved, moved, flat(features), flat(3 * features), flat(features)],
        out_shape=[
            jax.ShapeDtypeStruct(mid.shape, BF16),
            jax.ShapeDtypeStruct(mid.shape, BF16),
            jax.ShapeDtypeStruct((lat * rows, features), BF16),
            jax.ShapeDtypeStruct((lat * rows, 3 * features), BF16),
            jax.ShapeDtypeStruct((lat * rows, features), BF16),
        ],
        scratch_shapes=[
            pltpu.VMEM((rows, 3 * features), BF16),
            pltpu.VMEM((rows, features), BF16),
        ],
        compiler_params=pltpu.CompilerParams(vmem_limit_bytes=VMEM_LIMIT),
        name="temporal",
    )(mid, cot, gain, qkv, out)


def spatial_backward_kernel(
    dmid_ref, out_ref, qkv_ref, q_ref, kv_ref, p_ref,
    dq_ref, dkv_ref, own_ref, west_ref, east_ref,
    dproj_ref, acc_ref,
):
    _, lat, width, features = dmid_ref.shape
    rows = BH * width
    blocks = lat // BH
    step = 3 * rows
    dmid = dmid_ref[0].astype(F32).reshape(lat * width, features).astype(BF16)
    dproj_ref[...] = dot(dmid, out_ref[...], 1, 1).astype(BF16)
    mask = head_mask(rows)
    acc_ref[...] = jnp.zeros_like(acc_ref)
    offset = 0
    for b, (low, high) in enumerate(key_ranges(blocks, step)):
        span = high - low
        block = slice(b * rows, (b + 1) * rows)
        for g in range(features // LANES):
            lanes = slice(g * LANES, (g + 1) * LANES)
            late = slice(features + g * LANES, features + (g + 1) * LANES)
            queries = spread(q_ref[0, block, lanes], mask)
            d_out = spread(dproj_ref[block, lanes], mask)
            keys = kv_ref[0, low:high, lanes]
            values = kv_ref[0, low:high, late]
            weights = p_ref[0, g, offset : offset + span]
            wide = weights.astype(F32)
            d_weights = dot(values, d_out, 1, 1)
            delta = jnp.sum(wide * d_weights, axis=0, keepdims=True)
            d_scores = (wide * (d_weights - delta)).astype(BF16)
            d_query = gathered(dot(d_scores, keys, 0, 0), rows) * HDIM ** (-0.5)
            dq_ref[0, block, lanes] = d_query.astype(BF16)
            acc_ref[low:high, lanes] += dot(d_scores, queries)
            acc_ref[low:high, late] += dot(weights, d_out)
        offset += span
    dkv_ref[0] = acc_ref[...].astype(BF16)
    for b in range(blocks):
        part = slice(b * step, (b + 1) * step)
        d_y = dot(dkv_ref[0, part], qkv_ref[:, features:], 1, 1)
        block = slice(b * rows, (b + 1) * rows)
        d_own = d_y[rows : 2 * rows] + dot(dq_ref[0, block], qkv_ref[:, :features], 1, 1)
        for ref, value in ((west_ref, d_y[:rows]), (own_ref, d_own), (east_ref, d_y[2 * rows :])):
            ref[0, b * BH : (b + 1) * BH] = value.reshape(BH, width, features).astype(BF16)


def spatial_backward(dmid, out, qkv, q, kv, p):
    frames, lat, width, features = dmid.shape
    rows = lat * width
    outs = (
        (rows, features),
        (3 * rows, 2 * features),
        (lat, width, features),
        (lat, width, features),
        (lat, width, features),
    )
    return pl.pallas_call(
        spatial_backward_kernel,
        grid=(frames,),
        in_specs=[
            per_step((lat, width, features)),
            full(out.shape),
            full(qkv.shape),
            per_step(q.shape[1:]),
            per_step(kv.shape[1:]),
            per_step(p.shape[1:]),
        ],
        out_specs=[per_step(shape) for shape in outs],
        out_shape=[jax.ShapeDtypeStruct((frames,) + shape, BF16) for shape in outs],
        scratch_shapes=[
            pltpu.VMEM((rows, features), BF16),
            pltpu.VMEM((3 * rows, 2 * features), F32),
        ],
        compiler_params=pltpu.CompilerParams(vmem_limit_bytes=VMEM_LIMIT),
        name="spatial_backward",
    )(dmid, out, qkv, q, kv, p)


def final_kernel(tokens_ref, gain_ref, dmid_ref, own_ref, first_ref, second_ref, grad_ref):
    _, lat, width, features = tokens_ref.shape

    def flat(ref):
        return ref[0].astype(F32).reshape(lat * width, features)

    unit, inverse = normalized(flat(tokens_ref))
    d_y = flat(own_ref) + flat(first_ref) + flat(second_ref)
    grad = flat(dmid_ref) + norm_back(unit, inverse, gain_ref[...], d_y)
    grad_ref[0] = grad.reshape(lat, width, features)


def final_norm(tokens, gain, dmid, own, first, second):
    frames, lat, width, features = tokens.shape
    block = per_step((lat, width, features))
    return pl.pallas_call(
        final_kernel,
        grid=(frames,),
        in_specs=[block, full((1, features))] + [block] * 4,
        out_specs=block,
        out_shape=jax.ShapeDtypeStruct(tokens.shape, F32),
        compiler_params=pltpu.CompilerParams(vmem_limit_bytes=VMEM_LIMIT),
        name="final_norm",
    )(tokens, gain, dmid, own, first, second)


def exchanged_sum(parts, axis):
    arrived = lax.all_to_all(parts, axis, 0, 0, tiled=False)
    return jnp.sum(arrived.astype(F32), axis=0)


def scattered(term):
    columns = term.shape[1]
    cores = lax.axis_size("core")
    core = lax.axis_index("core")
    tiles = lax.axis_size(TILE)
    frames = lax.axis_size(FRAME)
    per_tile = term.shape[0] // tiles
    pairs = term.reshape(tiles // cores, cores, per_tile, columns)
    keep = lax.dynamic_index_in_dim(pairs, core, 1, keepdims=False)
    send = lax.dynamic_index_in_dim(pairs, 1 - core, 1, keepdims=False)
    got = lax.ppermute(send.astype(BF16), "core", [(0, 1), (1, 0)])
    mine = (keep.astype(F32) + got.astype(F32)).astype(BF16)
    summed = exchanged_sum(mine, ("xlo", "y")).astype(BF16)
    return exchanged_sum(summed.reshape(frames, per_tile // frames, columns), FRAME)


def shifted(shard, by):
    size = lax.axis_size(TILE)
    return lax.ppermute(shard, TILE, [(i, (i + by) % size) for i in range(size)])


def own_rows(weight):
    count = lax.axis_size(TILE + FRAME)
    per_device = weight.shape[0] // count
    at = lax.axis_index(TILE + FRAME) * per_device
    return lax.dynamic_slice_in_dim(weight, at, per_device, axis=0).astype(F32)


def finished(summed, qkv, gain, total):
    features, wide = qkv.shape
    d_qkv = summed[:, :wide]
    d_out = summed[:, wide:]
    scale = 1.0 / math.sqrt(total)
    d_gain = jnp.sum(own_rows(qkv) * d_qkv, axis=1) / own_rows(gain)
    return d_gain * scale, d_qkv * scale, d_out * scale


def shards(tokens, gain_space, qkv_space, out_space, gain_time, qkv_time, out_time, cotangent):
    frames, lat, width, features = tokens.shape
    total = frames * lat * width * lax.axis_size(TILE) * lax.axis_size(FRAME)
    gain_s = gain_space.reshape(1, features)
    gain_t = gain_time.reshape(1, features)

    def to_rows(shard):
        return lax.all_to_all(shard, FRAME, split_axis=1, concat_axis=0, tiled=True)

    def to_frames(shard):
        return lax.all_to_all(shard, FRAME, split_axis=0, concat_axis=1, tiled=True)

    west = shifted(tokens, 1)
    east = shifted(tokens, -1)
    cot_rows = to_rows(cotangent)
    y_s, q_s, kv_s, p_s, o_s, mid = spatial_forward(tokens, west, east, gain_s, qkv_space, out_space)
    layer_rows, dmid_rows, y_t, dpacked_t, o_t = temporal(
        to_rows(mid), cot_rows, gain_t, qkv_time, out_time
    )
    dmid = to_frames(dmid_rows)
    layer_out = to_frames(layer_rows)
    cot_flat = cot_rows.transpose(1, 0, 2, 3).reshape(-1, features)
    term_time = jnp.concatenate([dot(y_t, dpacked_t, 0, 0), dot(o_t, cot_flat, 0, 0)], axis=1)
    summed_time = scattered(term_time)
    dq, dkv, own, for_west, for_east = spatial_backward(dmid, out_space, qkv_space, q_s, kv_s, p_s)
    from_east = shifted(for_west, -1)
    from_west = shifted(for_east, 1)
    rows = lat * width
    y_ext = y_s.reshape(-1, features)
    y_own = y_s.reshape(frames, lat // BH, 3, BH * width, features)[:, :, 1].reshape(-1, features)
    term_space = jnp.concatenate(
        [
            dot(y_own, dq.reshape(-1, features), 0, 0),
            dot(y_ext, dkv.reshape(-1, 2 * features), 0, 0),
            dot(o_s.reshape(-1, features), dmid.reshape(-1, features), 0, 0),
        ],
        axis=1,
    )
    summed_space = scattered(term_space)
    grad_tokens = final_norm(tokens, gain_s, dmid, own, from_east, from_west)
    return (
        (layer_out, grad_tokens)
        + finished(summed_space, qkv_space, gain_space, total)
        + finished(summed_time, qkv_time, gain_time, total)
    )


def solution(mesh):
    fine = Mesh(mesh.devices.reshape(2, 4, 2, 4, 2), TILE + FRAME)
    token_spec = P(FRAME, None, TILE, None)
    row_spec = P(TILE + FRAME)
    return jax.shard_map(
        shards,
        mesh=fine,
        in_specs=(token_spec, P(), P(), P(), P(), P(), P(), token_spec),
        out_specs=(token_spec, token_spec) + (row_spec,) * 6,
        check_vma=False,
    )
```

```python
import functools
import math

import jax
import jax.numpy as jnp
from jax import lax
from jax.experimental import pallas as pl
from jax.experimental.pallas import tpu as pltpu
from jax.sharding import Mesh
from jax.sharding import PartitionSpec as P

HDIM = 64
BH = 8
LANES = 4 * HDIM
EPS = 1e-05
F32 = jnp.float32
BF16 = jnp.bfloat16
TILE = ("xlo", "y", "core")
FRAME = ("z", "xhi")
VMEM_LIMIT = 56 * 1024 * 1024


def dot(left, right, left_dim=1, right_dim=0):
    return lax.dot_general(
        left, right, (((left_dim,), (right_dim,)), ((), ())), preferred_element_type=F32
    )


def normalized(rows):
    centred = rows - jnp.mean(rows, axis=-1, keepdims=True)
    variance = jnp.mean(centred * centred, axis=-1, keepdims=True)
    inverse = lax.rsqrt(variance + EPS)
    return centred * inverse, inverse


def norm_back(unit, inverse, gain, d_out):
    d_unit = d_out * gain
    along = jnp.mean(d_unit * unit, axis=-1, keepdims=True)
    return inverse * (d_unit - jnp.mean(d_unit, axis=-1, keepdims=True) - unit * along)


def head_mask(rows):
    row_head = lax.broadcasted_iota(jnp.int32, (4 * rows, LANES), 0) // rows
    lane_head = lax.broadcasted_iota(jnp.int32, (4 * rows, LANES), 1) // HDIM
    return row_head == lane_head


def spread(group, mask):
    stacked = jnp.concatenate([group] * 4, axis=0)
    return jnp.where(mask, stacked, jnp.zeros_like(stacked))


def gathered(wide, rows):
    lane_head = lax.broadcasted_iota(jnp.int32, (rows, LANES), 1) // HDIM
    parts = [wide[h * rows : (h + 1) * rows] for h in range(4)]
    low = jnp.where(lane_head == 0, parts[0], parts[1])
    high = jnp.where(lane_head == 2, parts[2], parts[3])
    return jnp.where(lane_head < 2, low, high)


def softmax_rows(scores):
    top = jnp.max(scores, axis=0, keepdims=True)
    exponent = jnp.exp(scores - top)
    return exponent * (1.0 / jnp.sum(exponent, axis=0, keepdims=True))


def key_ranges(blocks, step):
    return [(max(b - 1, 0) * step, min(b + 2, blocks) * step) for b in range(blocks)]


def spatial_forward_kernel(
    own_ref, west_ref, east_ref, gain_ref, qkv_ref, out_ref,
    y_ref, q_ref, kv_ref, p_ref, o_ref, mid_ref,
):
    _, lat, width, features = own_ref.shape
    rows = BH * width
    blocks = lat // BH
    step = 3 * rows
    gain = gain_ref[...]
    for tile, ref in enumerate((west_ref, own_ref, east_ref)):
        wide = ref[0].astype(F32).reshape(lat * width, features)
        unit, _ = normalized(wide)
        y = (unit * gain).astype(BF16)
        for b in range(blocks):
            at = b * step + tile * rows
            y_ref[0, at : at + rows] = y[b * rows : (b + 1) * rows]
        if tile == 1:
            q_ref[0] = (dot(y, qkv_ref[:, :features]).astype(BF16) * HDIM ** (-0.5)).astype(BF16)
    for b in range(blocks):
        part = slice(b * step, (b + 1) * step)
        kv_ref[0, part] = dot(y_ref[0, part], qkv_ref[:, features:]).astype(BF16)
    mask = head_mask(rows)
    offset = 0
    for b, (low, high) in enumerate(key_ranges(blocks, step)):
        span = high - low
        for g in range(features // LANES):
            lanes = slice(g * LANES, (g + 1) * LANES)
            queries = spread(q_ref[0, b * rows : (b + 1) * rows, lanes], mask)
            keys = kv_ref[0, low:high, lanes]
            values = kv_ref[0, low:high, features + g * LANES : features + (g + 1) * LANES]
            weights = softmax_rows(dot(keys, queries, 1, 1)).astype(BF16)
            p_ref[0, g, offset : offset + span] = weights
            mixed = dot(weights, values, 0, 0)
            o_ref[0, b * rows : (b + 1) * rows, lanes] = gathered(mixed, rows).astype(BF16)
        offset += span
    wide = own_ref[0].astype(F32).reshape(lat * width, features)
    mid = wide + dot(o_ref[0], out_ref[...])
    mid_ref[:, 0] = mid.reshape(-1, mid_ref.shape[2], width, features).astype(BF16)


def full(shape):
    return pl.BlockSpec(shape, lambda *_: (0,) * len(shape))


def per_step(shape):
    return pl.BlockSpec((1,) + shape, lambda i: (i,) + (0,) * len(shape))


def cost(microseconds):
    return pl.CostEstimate(
        flops=microseconds * 10**9, bytes_accessed=4 << 20, transcendentals=2 * 10**6
    )


def grouped(peers, lat, width, features):
    return pl.BlockSpec((peers, 1, lat // peers, width, features), lambda i: (0, i, 0, 0, 0))


def spatial_forward(own, west, east, gain, qkv, out, peers):
    frames, lat, width, features = own.shape
    rows = lat * width
    blocks = lat // BH
    spans = sum(h - l for l, h in key_ranges(blocks, 3 * BH * width))
    groups = features // LANES
    outs = (
        ((3 * rows, features), BF16),
        ((rows, features), BF16),
        ((3 * rows, 2 * features), BF16),
        ((groups, spans, LANES), BF16),
        ((rows, features), BF16),
    )
    mid_shape = (peers, frames, lat // peers, width, features)
    return pl.pallas_call(
        spatial_forward_kernel,
        grid=(frames,),
        in_specs=[per_step((lat, width, features))] * 3
        + [full((1, features)), full(qkv.shape), full(out.shape)],
        out_specs=[per_step(shape) for shape, _ in outs] + [grouped(peers, lat, width, features)],
        out_shape=[jax.ShapeDtypeStruct((frames,) + shape, kind) for shape, kind in outs]
        + [jax.ShapeDtypeStruct(mid_shape, BF16)],
        compiler_params=pltpu.CompilerParams(vmem_limit_bytes=VMEM_LIMIT),
        cost_estimate=cost(14),
        name="spatial_forward",
    )(own, west, east, gain, qkv, out)


def temporal_kernel(
    mid_ref, cot_ref, gain_ref, qkv_ref, out_ref,
    layer_ref, dmid_ref, left_ref, right_ref,
    packed_ref, dproj_ref,
):
    peers, frames, _, width, features = mid_ref.shape
    rows = peers * frames * width
    gain = gain_ref[...]
    mid = mid_ref[:, :, 0].astype(F32).reshape(rows, features)
    cot = cot_ref[:, :, 0].astype(F32).reshape(rows, features)
    unit, inverse = normalized(mid)
    y = (unit * gain).astype(BF16)
    left_ref[:, :features] = y
    right_ref[:, 3 * features :] = cot.astype(BF16)
    packed_ref[...] = dot(y, qkv_ref[...]).astype(BF16)
    dproj_ref[...] = dot(cot.astype(BF16), out_ref[...], 1, 1).astype(BF16)
    mask = head_mask(rows)
    key_col = lax.broadcasted_iota(jnp.int32, (rows, 4 * rows), 0) % width
    query_col = lax.broadcasted_iota(jnp.int32, (rows, 4 * rows), 1) % width
    same = key_col == query_col
    scale = HDIM ** (-0.5)
    for g in range(features // LANES):
        lanes = [slice(s * features + g * LANES, s * features + (g + 1) * LANES) for s in range(3)]
        queries = spread((packed_ref[:, lanes[0]] * scale).astype(BF16), mask)
        keys = packed_ref[:, lanes[1]]
        values = packed_ref[:, lanes[2]]
        scores = jnp.where(same, dot(keys, queries, 1, 1), -1e30)
        wide = softmax_rows(scores)
        weights = wide.astype(BF16)
        mixed = dot(weights, values, 0, 0)
        o_lanes = slice(features + g * LANES, features + (g + 1) * LANES)
        left_ref[:, o_lanes] = gathered(mixed, rows).astype(BF16)
        d_out = spread(dproj_ref[:, lanes[0]], mask)
        d_weights = dot(values, d_out, 1, 1)
        delta = jnp.sum(wide * d_weights, axis=0, keepdims=True)
        d_scores = (wide * (d_weights - delta)).astype(BF16)
        d_query = gathered(dot(d_scores, keys, 0, 0), rows) * scale
        right_ref[:, lanes[0]] = d_query.astype(BF16)
        right_ref[:, lanes[1]] = dot(d_scores, queries).astype(BF16)
        right_ref[:, lanes[2]] = dot(weights, d_out).astype(BF16)
    layer = mid + dot(left_ref[:, features:], out_ref[...])
    layer_ref[:, :, 0] = layer.reshape(peers, frames, width, features).astype(BF16)
    d_y = dot(right_ref[:, : 3 * features], qkv_ref[...], 1, 1)
    d_mid = cot + norm_back(unit, inverse, gain, d_y)
    dmid_ref[:, :, 0] = d_mid.reshape(peers, frames, width, features).astype(BF16)


def temporal(mid, cot, gain, qkv, out):
    peers, frames, lat, width, features = mid.shape
    rows = peers * frames * width
    moved = pl.BlockSpec((peers, frames, 1, width, features), lambda i: (0, 0, i, 0, 0))

    def flat(columns):
        return pl.BlockSpec((rows, columns), lambda i: (i, 0))

    return pl.pallas_call(
        temporal_kernel,
        grid=(lat,),
        in_specs=[moved, moved, full((1, features)), full(qkv.shape), full(out.shape)],
        out_specs=[moved, moved, flat(2 * features), flat(4 * features)],
        out_shape=[
            jax.ShapeDtypeStruct(mid.shape, BF16),
            jax.ShapeDtypeStruct(mid.shape, BF16),
            jax.ShapeDtypeStruct((lat * rows, 2 * features), BF16),
            jax.ShapeDtypeStruct((lat * rows, 4 * features), BF16),
        ],
        scratch_shapes=[
            pltpu.VMEM((rows, 3 * features), BF16),
            pltpu.VMEM((rows, features), BF16),
        ],
        compiler_params=pltpu.CompilerParams(vmem_limit_bytes=VMEM_LIMIT),
        cost_estimate=cost(18),
        name="temporal",
    )(mid, cot, gain, qkv, out)


def spatial_backward_kernel(
    dmid_ref, out_ref, qkv_ref, q_ref, kv_ref, p_ref,
    dq_ref, dkv_ref, own_ref, west_ref, east_ref,
    dproj_ref, acc_ref,
):
    _, lat, width, features = own_ref.shape
    rows = BH * width
    blocks = lat // BH
    step = 3 * rows
    dmid = dmid_ref[...].astype(F32).reshape(lat * width, features).astype(BF16)
    dproj_ref[...] = dot(dmid, out_ref[...], 1, 1).astype(BF16)
    mask = head_mask(rows)
    acc_ref[...] = jnp.zeros_like(acc_ref)
    offset = 0
    for b, (low, high) in enumerate(key_ranges(blocks, step)):
        span = high - low
        block = slice(b * rows, (b + 1) * rows)
        for g in range(features // LANES):
            lanes = slice(g * LANES, (g + 1) * LANES)
            late = slice(features + g * LANES, features + (g + 1) * LANES)
            queries = spread(q_ref[0, block, lanes], mask)
            d_out = spread(dproj_ref[block, lanes], mask)
            keys = kv_ref[0, low:high, lanes]
            values = kv_ref[0, low:high, late]
            weights = p_ref[0, g, offset : offset + span]
            wide = weights.astype(F32)
            d_weights = dot(values, d_out, 1, 1)
            delta = jnp.sum(wide * d_weights, axis=0, keepdims=True)
            d_scores = (wide * (d_weights - delta)).astype(BF16)
            d_query = gathered(dot(d_scores, keys, 0, 0), rows) * HDIM ** (-0.5)
            dq_ref[0, block, lanes] = d_query.astype(BF16)
            acc_ref[low:high, lanes] += dot(d_scores, queries)
            acc_ref[low:high, late] += dot(weights, d_out)
        offset += span
    dkv_ref[0] = acc_ref[...].astype(BF16)
    for b in range(blocks):
        part = slice(b * step, (b + 1) * step)
        d_y = dot(dkv_ref[0, part], qkv_ref[:, features:], 1, 1)
        block = slice(b * rows, (b + 1) * rows)
        d_own = d_y[rows : 2 * rows] + dot(dq_ref[0, block], qkv_ref[:, :features], 1, 1)
        for ref, value in ((west_ref, d_y[:rows]), (own_ref, d_own), (east_ref, d_y[2 * rows :])):
            ref[0, b * BH : (b + 1) * BH] = value.reshape(BH, width, features).astype(BF16)


def spatial_backward(dmid, out, qkv, q, kv, p):
    peers, frames, each, width, features = dmid.shape
    lat = peers * each
    rows = lat * width
    outs = (
        (rows, features),
        (3 * rows, 2 * features),
        (lat, width, features),
        (lat, width, features),
        (lat, width, features),
    )
    return pl.pallas_call(
        spatial_backward_kernel,
        grid=(frames,),
        in_specs=[
            grouped(peers, lat, width, features),
            full(out.shape),
            full(qkv.shape),
            per_step(q.shape[1:]),
            per_step(kv.shape[1:]),
            per_step(p.shape[1:]),
        ],
        out_specs=[per_step(shape) for shape in outs],
        out_shape=[jax.ShapeDtypeStruct((frames,) + shape, BF16) for shape in outs],
        scratch_shapes=[
            pltpu.VMEM((rows, features), BF16),
            pltpu.VMEM((3 * rows, 2 * features), F32),
        ],
        compiler_params=pltpu.CompilerParams(vmem_limit_bytes=VMEM_LIMIT),
        cost_estimate=cost(20),
        name="spatial_backward",
    )(dmid, out, qkv, q, kv, p)


def final_kernel(tokens_ref, gain_ref, dmid_ref, own_ref, first_ref, second_ref, grad_ref):
    _, lat, width, features = tokens_ref.shape

    def flat(ref):
        return ref[0].astype(F32).reshape(lat * width, features)

    unit, inverse = normalized(flat(tokens_ref))
    d_y = flat(own_ref) + flat(first_ref) + flat(second_ref)
    d_mid = dmid_ref[...].astype(F32).reshape(lat * width, features)
    grad = d_mid + norm_back(unit, inverse, gain_ref[...], d_y)
    grad_ref[0] = grad.reshape(lat, width, features)


def final_norm(tokens, gain, dmid, own, first, second):
    frames, lat, width, features = tokens.shape
    block = per_step((lat, width, features))
    return pl.pallas_call(
        final_kernel,
        grid=(frames,),
        in_specs=[block, full((1, features)), grouped(dmid.shape[0], lat, width, features)]
        + [block] * 3,
        out_specs=block,
        out_shape=jax.ShapeDtypeStruct(tokens.shape, F32),
        compiler_params=pltpu.CompilerParams(vmem_limit_bytes=VMEM_LIMIT),
        cost_estimate=cost(3),
        name="final_norm",
    )(tokens, gain, dmid, own, first, second)


def split_store(core_ref, term, keep_ref, send_ref, ring=1):
    tiles, rows, columns = keep_ref.shape
    pairs = term.reshape(tiles, 2, rows, columns)
    first = core_ref[0] == 0
    for tile in range(tiles):
        at = tile % ring * (tiles // ring) + tile // ring
        even, odd = pairs[tile, 0], pairs[tile, 1]
        keep_ref[at] = jnp.where(first, even, odd).astype(BF16)
        send_ref[at] = jnp.where(first, odd, even).astype(BF16)


def term_time_kernel(ring, core_ref, left_ref, right_ref, keep_ref, send_ref):
    split_store(core_ref, dot(left_ref[...], right_ref[...], 0, 0), keep_ref, send_ref, ring)


def split_call(kernel, core, operands, specs, features, tiles, name, flops):
    shape = (tiles, features // (2 * tiles), 4 * features)
    block = pl.BlockSpec(shape[:2] + (features,), lambda i, core: (0, 0, i))
    return pl.pallas_call(
        kernel,
        grid_spec=pltpu.PrefetchScalarGridSpec(
            num_scalar_prefetch=1, grid=(4,), in_specs=specs, out_specs=[block, block]
        ),
        out_shape=[jax.ShapeDtypeStruct(shape, BF16)] * 2,
        compiler_params=pltpu.CompilerParams(vmem_limit_bytes=VMEM_LIMIT),
        cost_estimate=pl.CostEstimate(flops=flops, bytes_accessed=12 << 20, transcendentals=0),
        name=name,
    )(core, *operands)


def term_time(core, left, right, tiles, ring):
    rows, double = left.shape
    features = double // 2
    specs = [
        pl.BlockSpec((rows, features), lambda i, core: (0, i // 3)),
        pl.BlockSpec((rows, features), lambda i, core: (0, i)),
    ]
    return split_call(
        functools.partial(term_time_kernel, ring), core, (left, right), specs, features, tiles,
        "term_time", 2 * 10**9,
    )


def term_space_kernel(core_ref, y_ref, dq_ref, dkv_ref, o_ref, dmid_ref, keep_ref, send_ref):
    step = pl.program_id(0)
    frames, ext, features = y_ref.shape
    own = dq_ref.shape[1]

    @pl.when(step == 0)
    def _():
        part = BH * dmid_ref.shape[3]
        blocks = own // part
        pieces = [
            y_ref[f, (3 * b + 1) * part : (3 * b + 2) * part]
            for f in range(frames)
            for b in range(blocks)
        ]
        left = jnp.concatenate(pieces, axis=0)
        right = dq_ref[...].reshape(frames * own, features)
        split_store(core_ref, dot(left, right, 0, 0), keep_ref, send_ref)

    @pl.when((step == 1) | (step == 2))
    def _():
        left = y_ref[...].reshape(frames * ext, features)
        right = dkv_ref[...].reshape(frames * ext, features)
        split_store(core_ref, dot(left, right, 0, 0), keep_ref, send_ref)

    @pl.when(step == 3)
    def _():
        left = o_ref[...].reshape(frames * own, features)
        right = [dmid_ref[:, f].astype(F32).reshape(own, features) for f in range(frames)]
        right = jnp.concatenate(right, axis=0).astype(BF16)
        split_store(core_ref, dot(left, right, 0, 0), keep_ref, send_ref)


def term_space(core, y, dq, dkv, o, dmid, tiles):
    features = y.shape[-1]

    def whole(array):
        return pl.BlockSpec(array.shape, lambda i, core: (0,) * array.ndim)

    specs = [
        whole(y),
        whole(dq),
        pl.BlockSpec(dkv.shape[:2] + (features,), lambda i, core: (0, 0, jnp.clip(i - 1, 0, 1))),
        whole(o),
        whole(dmid),
    ]
    return split_call(
        term_space_kernel, core, (y, dq, dkv, o, dmid), specs, features, tiles, "term_space",
        4 * 10**9,
    )


def paired(keep, send):
    got = lax.ppermute(send, "core", [(0, 1), (1, 0)])
    return (keep.astype(F32) + got.astype(F32)).astype(BF16)


def folded(array, *lead):
    return array.reshape(lead + (-1, 128))


def ring_sum(chunks, axis):
    size = lax.axis_size(axis)
    me = lax.axis_index(axis).astype(jnp.uint32)

    def chunk(by):
        at = lax.bitwise_and(me + jnp.uint32(by), jnp.uint32(size - 1))
        return lax.dynamic_index_in_dim(chunks, at, 0, keepdims=False)

    total = chunk(0).astype(F32)
    for by in range(1, size):
        moved = lax.ppermute(chunk(by), axis, [(i, (i + by) % size) for i in range(size)])
        total = total + moved.astype(F32)
    return total


def summed_over_y(mine):
    return lax.psum_scatter(
        mine.reshape(-1, mine.shape[-1]), "y", scatter_dimension=0, tiled=True
    )


def summed_over_zx(part):
    halves, z, xhi = lax.axis_size("xlo"), lax.axis_size("z"), lax.axis_size("xhi")
    pieces = folded(part, halves, z, xhi).transpose(1, 0, 2, 3, 4)
    after_z = ring_sum(pieces, "z").astype(BF16)
    return ring_sum(after_z.reshape((halves * xhi,) + after_z.shape[2:]), ("xlo", "xhi"))


def summed_at_once(mine):
    rest = ("xlo", "y", "z", "xhi")
    count = lax.axis_size(rest)
    arrived = lax.all_to_all(folded(mine, count), rest, 0, 0, tiled=False)
    return jnp.sum(arrived.astype(F32), axis=0)


def shifted(shard, by):
    size = lax.axis_size(TILE)
    return lax.ppermute(shard, TILE, [(i, (i + by) % size) for i in range(size)])


def own_rows(weight):
    count = lax.axis_size(TILE + FRAME)
    per_device = weight.shape[0] // count
    at = lax.axis_index(TILE + FRAME) * per_device
    return lax.dynamic_slice_in_dim(weight, at, per_device, axis=0).astype(F32)


def finished(total, qkv, gain, tokens):
    features, wide = qkv.shape
    summed = total.reshape(-1, wide + features) * (1.0 / math.sqrt(tokens))
    d_qkv = summed[:, :wide]
    d_gain = jnp.sum(own_rows(qkv) * d_qkv, axis=1) / own_rows(gain)
    return d_gain, d_qkv, summed[:, wide:]


def shards(tokens, gain_space, qkv_space, out_space, gain_time, qkv_time, out_time, cotangent):
    frames, lat, width, features = tokens.shape
    total = frames * lat * width * lax.axis_size(TILE) * lax.axis_size(FRAME)
    gain_s = gain_space.reshape(1, features)
    gain_t = gain_time.reshape(1, features)
    core = lax.axis_index("core").astype(jnp.int32).reshape(1)
    tiles = lax.axis_size(("xlo", "y"))

    peers = lax.axis_size(FRAME)

    def exchanged(chunks):
        return lax.all_to_all(chunks, FRAME, 0, 0, tiled=False)

    west = shifted(tokens, 1)
    east = shifted(tokens, -1)
    cot_chunks = cotangent.reshape(frames, peers, lat // peers, width, features)
    cot_rows = exchanged(cot_chunks.transpose(1, 0, 2, 3, 4))
    y_s, q_s, kv_s, p_s, o_s, mid = spatial_forward(
        tokens, west, east, gain_s, qkv_space, out_space, peers
    )
    layer_rows, dmid_rows, left_t, right_t = temporal(
        exchanged(mid), cot_rows, gain_t, qkv_time, out_time
    )
    dmid = exchanged(dmid_rows)
    keep_t, send_t = term_time(core, left_t, right_t, tiles, lax.axis_size("y"))
    mine_t = paired(keep_t, send_t)
    dmid, mine_t, layer_rows = lax.optimization_barrier((dmid, mine_t, layer_rows))
    part_t = summed_over_y(mine_t)
    layer_chunks = exchanged(layer_rows)
    dq, dkv, own, for_west, for_east = spatial_backward(dmid, out_space, qkv_space, q_s, kv_s, p_s)
    from_east = shifted(for_west, -1)
    from_west = shifted(for_east, 1)
    keep_s, send_s = term_space(core, y_s, dq, dkv, o_s, dmid, tiles)
    send_s, layer_chunks = lax.optimization_barrier((send_s, layer_chunks))
    mine_s = paired(keep_s, send_s)
    mine_s, part_t = lax.optimization_barrier((mine_s, part_t))
    summed_space = summed_at_once(mine_s)
    summed_time = summed_over_zx(part_t)
    layer_out = layer_chunks.transpose(1, 0, 2, 3, 4).reshape(tokens.shape)
    grad_tokens = final_norm(tokens, gain_s, dmid, own, from_east, from_west)
    return (
        (layer_out, grad_tokens)
        + finished(summed_space, qkv_space, gain_space, total)
        + finished(summed_time, qkv_time, gain_time, total)
    )


def solution(mesh):
    fine = Mesh(mesh.devices.reshape(2, 4, 2, 4, 2), TILE + FRAME)
    token_spec = P(FRAME, None, TILE, None)
    row_spec = P(TILE + FRAME)
    return jax.shard_map(
        shards,
        mesh=fine,
        in_specs=(token_spec, P(), P(), P(), P(), P(), P(), token_spec),
        out_specs=(token_spec, token_spec) + (row_spec,) * 6,
        check_vma=False,
    )
```

```python
import math

import jax
import jax.numpy as jnp
from jax import lax
from jax.experimental import pallas as pl
from jax.experimental.pallas import tpu as pltpu
from jax.sharding import Mesh
from jax.sharding import PartitionSpec as P

HDIM = 64
BH = 8
LANES = 4 * HDIM
EPS = 1e-05
F32 = jnp.float32
BF16 = jnp.bfloat16
TILE = ("xlo", "y", "core")
FRAME = ("z", "xhi")
VMEM_LIMIT = 56 * 1024 * 1024


def dot(left, right, left_dim=1, right_dim=0):
    return lax.dot_general(
        left, right, (((left_dim,), (right_dim,)), ((), ())), preferred_element_type=F32
    )


def normalized(rows):
    centred = rows - jnp.mean(rows, axis=-1, keepdims=True)
    variance = jnp.mean(centred * centred, axis=-1, keepdims=True)
    inverse = lax.rsqrt(variance + EPS)
    return centred * inverse, inverse


def norm_back(unit, inverse, gain, d_out):
    d_unit = d_out * gain
    along = jnp.mean(d_unit * unit, axis=-1, keepdims=True)
    return inverse * (d_unit - jnp.mean(d_unit, axis=-1, keepdims=True) - unit * along)


def head_mask(rows):
    row_head = lax.broadcasted_iota(jnp.int32, (4 * rows, LANES), 0) // rows
    lane_head = lax.broadcasted_iota(jnp.int32, (4 * rows, LANES), 1) // HDIM
    return row_head == lane_head


def spread(group, mask):
    stacked = jnp.concatenate([group] * 4, axis=0)
    return jnp.where(mask, stacked, jnp.zeros_like(stacked))


def gathered(wide, rows):
    lane_head = lax.broadcasted_iota(jnp.int32, (rows, LANES), 1) // HDIM
    parts = [wide[h * rows : (h + 1) * rows] for h in range(4)]
    low = jnp.where(lane_head == 0, parts[0], parts[1])
    high = jnp.where(lane_head == 2, parts[2], parts[3])
    return jnp.where(lane_head < 2, low, high)


def softmax_rows(scores):
    top = jnp.max(scores, axis=0, keepdims=True)
    exponent = jnp.exp(scores - top)
    return exponent * (1.0 / jnp.sum(exponent, axis=0, keepdims=True))


def key_ranges(blocks, step):
    return [(max(b - 1, 0) * step, min(b + 2, blocks) * step) for b in range(blocks)]


def spatial_forward_kernel(
    own_ref, west_ref, east_ref, gain_ref, qkv_ref, out_ref,
    y_ref, q_ref, kv_ref, p_ref, o_ref, mid_ref,
):
    _, lat, width, features = own_ref.shape
    rows = BH * width
    blocks = lat // BH
    step = 3 * rows
    gain = gain_ref[...]
    for tile, ref in enumerate((west_ref, own_ref, east_ref)):
        wide = ref[0].astype(F32).reshape(lat * width, features)
        unit, _ = normalized(wide)
        y = (unit * gain).astype(BF16)
        for b in range(blocks):
            at = b * step + tile * rows
            y_ref[0, at : at + rows] = y[b * rows : (b + 1) * rows]
        if tile == 1:
            q_ref[0] = (dot(y, qkv_ref[:, :features]).astype(BF16) * HDIM ** (-0.5)).astype(BF16)
    for b in range(blocks):
        part = slice(b * step, (b + 1) * step)
        kv_ref[0, part] = dot(y_ref[0, part], qkv_ref[:, features:]).astype(BF16)
    mask = head_mask(rows)
    offset = 0
    for b, (low, high) in enumerate(key_ranges(blocks, step)):
        span = high - low
        for g in range(features // LANES):
            lanes = slice(g * LANES, (g + 1) * LANES)
            queries = spread(q_ref[0, b * rows : (b + 1) * rows, lanes], mask)
            keys = kv_ref[0, low:high, lanes]
            values = kv_ref[0, low:high, features + g * LANES : features + (g + 1) * LANES]
            weights = softmax_rows(dot(keys, queries, 1, 1)).astype(BF16)
            p_ref[0, g, offset : offset + span] = weights
            mixed = dot(weights, values, 0, 0)
            o_ref[0, b * rows : (b + 1) * rows, lanes] = gathered(mixed, rows).astype(BF16)
        offset += span
    wide = own_ref[0].astype(F32).reshape(lat * width, features)
    mid = wide + dot(o_ref[0], out_ref[...])
    mid_ref[:, 0] = mid.reshape(-1, mid_ref.shape[2], width, features).astype(BF16)


def full(shape):
    return pl.BlockSpec(shape, lambda *_: (0,) * len(shape))


def per_step(shape):
    return pl.BlockSpec((1,) + shape, lambda i: (i,) + (0,) * len(shape))


def cost(microseconds):
    return pl.CostEstimate(
        flops=microseconds * 10**9, bytes_accessed=4 << 20, transcendentals=2 * 10**6
    )


def grouped(peers, lat, width, features):
    return pl.BlockSpec((peers, 1, lat // peers, width, features), lambda i: (0, i, 0, 0, 0))


def spatial_forward(own, west, east, gain, qkv, out, peers):
    frames, lat, width, features = own.shape
    rows = lat * width
    blocks = lat // BH
    spans = sum(h - l for l, h in key_ranges(blocks, 3 * BH * width))
    groups = features // LANES
    outs = (
        ((3 * rows, features), BF16),
        ((rows, features), BF16),
        ((3 * rows, 2 * features), BF16),
        ((groups, spans, LANES), BF16),
        ((rows, features), BF16),
    )
    mid_shape = (peers, frames, lat // peers, width, features)
    return pl.pallas_call(
        spatial_forward_kernel,
        grid=(frames,),
        in_specs=[per_step((lat, width, features))] * 3
        + [full((1, features)), full(qkv.shape), full(out.shape)],
        out_specs=[per_step(shape) for shape, _ in outs] + [grouped(peers, lat, width, features)],
        out_shape=[jax.ShapeDtypeStruct((frames,) + shape, kind) for shape, kind in outs]
        + [jax.ShapeDtypeStruct(mid_shape, BF16)],
        compiler_params=pltpu.CompilerParams(vmem_limit_bytes=VMEM_LIMIT),
        cost_estimate=cost(14),
        name="spatial_forward",
    )(own, west, east, gain, qkv, out)


def temporal_kernel(
    mid_ref, cot_ref, gain_ref, qkv_ref, out_ref,
    both_ref, left_ref, right_ref,
    packed_ref, dproj_ref,
):
    peers, frames, lat, width, features = mid_ref.shape
    rows = peers * frames * width
    gain = gain_ref[...]
    scale = HDIM ** (-0.5)

    def by_row(ref, row):
        return ref[:, :, row].astype(F32).reshape(rows, features)

    for row in range(lat):
        part = slice(row * rows, (row + 1) * rows)
        unit, _ = normalized(by_row(mid_ref, row))
        left_ref[part, :features] = (unit * gain).astype(BF16)
        right_ref[part, 3 * features :] = by_row(cot_ref, row).astype(BF16)
    packed_ref[...] = dot(left_ref[:, :features], qkv_ref[...]).astype(BF16)
    dproj_ref[...] = dot(right_ref[:, 3 * features :], out_ref[...], 1, 1).astype(BF16)
    mask = head_mask(rows)
    key_col = lax.broadcasted_iota(jnp.int32, (rows, 4 * rows), 0) % width
    query_col = lax.broadcasted_iota(jnp.int32, (rows, 4 * rows), 1) % width
    same = key_col == query_col
    for row in range(lat):
        part = slice(row * rows, (row + 1) * rows)
        for g in range(features // LANES):
            lanes = [
                slice(s * features + g * LANES, s * features + (g + 1) * LANES) for s in range(3)
            ]
            queries = spread((packed_ref[part, lanes[0]] * scale).astype(BF16), mask)
            keys = packed_ref[part, lanes[1]]
            values = packed_ref[part, lanes[2]]
            scores = jnp.where(same, dot(keys, queries, 1, 1), -1e30)
            wide = softmax_rows(scores)
            weights = wide.astype(BF16)
            mixed = dot(weights, values, 0, 0)
            left_ref[part, lanes[1]] = gathered(mixed, rows).astype(BF16)
            d_out = spread(dproj_ref[part, lanes[0]], mask)
            d_weights = dot(values, d_out, 1, 1)
            delta = jnp.sum(wide * d_weights, axis=0, keepdims=True)
            d_scores = (wide * (d_weights - delta)).astype(BF16)
            d_query = gathered(dot(d_scores, keys, 0, 0), rows) * scale
            right_ref[part, lanes[0]] = d_query.astype(BF16)
            right_ref[part, lanes[1]] = dot(d_scores, queries).astype(BF16)
            right_ref[part, lanes[2]] = dot(weights, d_out).astype(BF16)
    layer = dot(left_ref[:, features:], out_ref[...])
    d_y = dot(right_ref[:, : 3 * features], qkv_ref[...], 1, 1)
    shape = (peers, frames, width, features)
    for row in range(lat):
        part = slice(row * rows, (row + 1) * rows)
        mid = by_row(mid_ref, row)
        unit, inverse = normalized(mid)
        d_mid = by_row(cot_ref, row) + norm_back(unit, inverse, gain, d_y[part])
        both_ref[:, :frames, row] = d_mid.reshape(shape).astype(BF16)
        both_ref[:, frames:, row] = (mid + layer[part]).reshape(shape).astype(BF16)


def temporal(mid, cot, gain, qkv, out):
    peers, frames, lat, width, features = mid.shape
    rows = peers * frames * lat * width
    return pl.pallas_call(
        temporal_kernel,
        out_shape=[
            jax.ShapeDtypeStruct((peers, 2 * frames, lat, width, features), BF16),
            jax.ShapeDtypeStruct((rows, 2 * features), BF16),
            jax.ShapeDtypeStruct((rows, 4 * features), BF16),
        ],
        scratch_shapes=[
            pltpu.VMEM((rows, 3 * features), BF16),
            pltpu.VMEM((rows, features), BF16),
        ],
        compiler_params=pltpu.CompilerParams(vmem_limit_bytes=VMEM_LIMIT),
        cost_estimate=cost(18),
        name="temporal",
    )(mid, cot, gain, qkv, out)


def back_projection_kernel(dmid_ref, out_ref, dproj_ref):
    rows, features = dproj_ref.shape[1:]
    dmid = dmid_ref[...].astype(F32).reshape(rows, features).astype(BF16)
    dproj_ref[0] = dot(dmid, out_ref[...], 1, 1).astype(BF16)


def back_projection(dmid, out, frames):
    peers, _, each, width, features = dmid.shape
    rows = peers * each * width
    return pl.pallas_call(
        back_projection_kernel,
        grid=(frames,),
        in_specs=[grouped(peers, peers * each, width, features), full(out.shape)],
        out_specs=per_step((rows, features)),
        out_shape=jax.ShapeDtypeStruct((frames, rows, features), BF16),
        compiler_params=pltpu.CompilerParams(vmem_limit_bytes=VMEM_LIMIT),
        cost_estimate=cost(30),
        name="back_projection",
    )(dmid, out)


def spatial_backward_kernel(
    dproj_ref, qkv_ref, q_ref, kv_ref, p_ref,
    dq_ref, dkv_ref, own_ref, west_ref, east_ref,
    acc_ref,
):
    _, lat, width, features = own_ref.shape
    rows = BH * width
    blocks = lat // BH
    step = 3 * rows
    mask = head_mask(rows)
    acc_ref[...] = jnp.zeros_like(acc_ref)
    offset = 0
    for b, (low, high) in enumerate(key_ranges(blocks, step)):
        span = high - low
        block = slice(b * rows, (b + 1) * rows)
        for g in range(features // LANES):
            lanes = slice(g * LANES, (g + 1) * LANES)
            late = slice(features + g * LANES, features + (g + 1) * LANES)
            queries = spread(q_ref[0, block, lanes], mask)
            d_out = spread(dproj_ref[0, block, lanes], mask)
            keys = kv_ref[0, low:high, lanes]
            values = kv_ref[0, low:high, late]
            weights = p_ref[0, g, offset : offset + span]
            wide = weights.astype(F32)
            d_weights = dot(values, d_out, 1, 1)
            delta = jnp.sum(wide * d_weights, axis=0, keepdims=True)
            d_scores = (wide * (d_weights - delta)).astype(BF16)
            d_query = gathered(dot(d_scores, keys, 0, 0), rows) * HDIM ** (-0.5)
            dq_ref[0, block, lanes] = d_query.astype(BF16)
            acc_ref[low:high, lanes] += dot(d_scores, queries)
            acc_ref[low:high, late] += dot(weights, d_out)
        offset += span
    dkv_ref[0] = acc_ref[...].astype(BF16)
    for b in range(blocks):
        part = slice(b * step, (b + 1) * step)
        d_y = dot(dkv_ref[0, part], qkv_ref[:, features:], 1, 1)
        block = slice(b * rows, (b + 1) * rows)
        d_own = d_y[rows : 2 * rows] + dot(dq_ref[0, block], qkv_ref[:, :features], 1, 1)
        for ref, value in ((west_ref, d_y[:rows]), (own_ref, d_own), (east_ref, d_y[2 * rows :])):
            ref[0, b * BH : (b + 1) * BH] = value.reshape(BH, width, features).astype(BF16)


def spatial_backward(dproj, qkv, q, kv, p, lat):
    frames, rows, features = dproj.shape
    width = rows // lat
    outs = (
        (rows, features),
        (3 * rows, 2 * features),
        (lat, width, features),
        (lat, width, features),
        (lat, width, features),
    )
    return pl.pallas_call(
        spatial_backward_kernel,
        grid=(frames,),
        in_specs=[
            per_step((rows, features)),
            full(qkv.shape),
            per_step(q.shape[1:]),
            per_step(kv.shape[1:]),
            per_step(p.shape[1:]),
        ],
        out_specs=[per_step(shape) for shape in outs],
        out_shape=[jax.ShapeDtypeStruct((frames,) + shape, BF16) for shape in outs],
        scratch_shapes=[
            pltpu.VMEM((3 * rows, 2 * features), F32),
        ],
        compiler_params=pltpu.CompilerParams(vmem_limit_bytes=VMEM_LIMIT),
        cost_estimate=cost(20),
        name="spatial_backward",
    )(dproj, qkv, q, kv, p)


def final_kernel(tokens_ref, gain_ref, dmid_ref, own_ref, first_ref, second_ref, grad_ref):
    _, lat, width, features = tokens_ref.shape

    def flat(ref):
        return ref[0].astype(F32).reshape(lat * width, features)

    unit, inverse = normalized(flat(tokens_ref))
    d_y = flat(own_ref) + flat(first_ref) + flat(second_ref)
    d_mid = dmid_ref[...].astype(F32).reshape(lat * width, features)
    grad = d_mid + norm_back(unit, inverse, gain_ref[...], d_y)
    grad_ref[0] = grad.reshape(lat, width, features)


def final_norm(tokens, gain, dmid, own, first, second):
    frames, lat, width, features = tokens.shape
    block = per_step((lat, width, features))
    return pl.pallas_call(
        final_kernel,
        grid=(frames,),
        in_specs=[block, full((1, features)), grouped(dmid.shape[0], lat, width, features)]
        + [block] * 3,
        out_specs=block,
        out_shape=jax.ShapeDtypeStruct(tokens.shape, F32),
        compiler_params=pltpu.CompilerParams(vmem_limit_bytes=VMEM_LIMIT),
        cost_estimate=cost(3),
        name="final_norm",
    )(tokens, gain, dmid, own, first, second)


def split_store(core_ref, term, keep_ref, send_ref):
    tiles, rows, columns = keep_ref.shape
    pairs = term.reshape(tiles, 2, rows, columns)
    first = core_ref[0] == 0
    for tile in range(tiles):
        even, odd = pairs[tile, 0], pairs[tile, 1]
        keep_ref[tile] = jnp.where(first, even, odd).astype(BF16)
        send_ref[tile] = jnp.where(first, odd, even).astype(BF16)


def term_time_kernel(core_ref, left_ref, right_ref, keep_ref, send_ref):
    split_store(core_ref, dot(left_ref[...], right_ref[...], 0, 0), keep_ref, send_ref)


def split_call(kernel, core, operands, specs, features, tiles, name, flops):
    shape = (tiles, features // (2 * tiles), 4 * features)
    block = pl.BlockSpec(shape[:2] + (features,), lambda i, core: (0, 0, i))
    return pl.pallas_call(
        kernel,
        grid_spec=pltpu.PrefetchScalarGridSpec(
            num_scalar_prefetch=1, grid=(4,), in_specs=specs, out_specs=[block, block]
        ),
        out_shape=[jax.ShapeDtypeStruct(shape, BF16)] * 2,
        compiler_params=pltpu.CompilerParams(vmem_limit_bytes=VMEM_LIMIT),
        cost_estimate=pl.CostEstimate(flops=flops, bytes_accessed=1, transcendentals=0),
        name=name,
    )(core, *operands)


def term_time(core, left, right, tiles):
    rows, double = left.shape
    features = double // 2
    specs = [
        pl.BlockSpec((rows, features), lambda i, core: (0, i // 3)),
        pl.BlockSpec((rows, features), lambda i, core: (0, i)),
    ]
    return split_call(
        term_time_kernel, core, (left, right), specs, features, tiles,
        "term_time", 1,
    )


def term_space_kernel(core_ref, y_ref, dq_ref, dkv_ref, o_ref, dmid_ref, keep_ref, send_ref):
    step = pl.program_id(0)
    frames, ext, features = y_ref.shape
    own = dq_ref.shape[1]

    @pl.when(step == 0)
    def _():
        part = BH * dmid_ref.shape[3]
        blocks = own // part
        pieces = [
            y_ref[f, (3 * b + 1) * part : (3 * b + 2) * part]
            for f in range(frames)
            for b in range(blocks)
        ]
        left = jnp.concatenate(pieces, axis=0)
        right = dq_ref[...].reshape(frames * own, features)
        split_store(core_ref, dot(left, right, 0, 0), keep_ref, send_ref)

    @pl.when((step == 1) | (step == 2))
    def _():
        left = y_ref[...].reshape(frames * ext, features)
        right = dkv_ref[...].reshape(frames * ext, features)
        split_store(core_ref, dot(left, right, 0, 0), keep_ref, send_ref)

    @pl.when(step == 3)
    def _():
        left = o_ref[...].reshape(frames * own, features)
        right = [dmid_ref[:, f].astype(F32).reshape(own, features) for f in range(frames)]
        right = jnp.concatenate(right, axis=0).astype(BF16)
        split_store(core_ref, dot(left, right, 0, 0), keep_ref, send_ref)


def term_space(core, y, dq, dkv, o, dmid, tiles):
    features = y.shape[-1]

    def whole(array):
        return pl.BlockSpec(array.shape, lambda i, core: (0,) * array.ndim)

    specs = [
        whole(y),
        whole(dq),
        pl.BlockSpec(dkv.shape[:2] + (features,), lambda i, core: (0, 0, jnp.clip(i - 1, 0, 1))),
        whole(o),
        pl.BlockSpec(
            (dmid.shape[0], y.shape[0]) + dmid.shape[2:], lambda i, core: (0,) * dmid.ndim
        ),
    ]
    return split_call(
        term_space_kernel, core, (y, dq, dkv, o, dmid), specs, features, tiles, "term_space", 1,
    )


def add_kernel(left_ref, right_ref, sum_ref):
    sum_ref[...] = (left_ref[...].astype(F32) + right_ref[...].astype(F32)).astype(BF16)


def paired(keep, send):
    got = lax.ppermute(send, "core", [(0, 1), (1, 0)])
    block = pl.BlockSpec((1,) + keep.shape[1:], lambda i: (i, 0, 0))
    return pl.pallas_call(
        add_kernel,
        grid=(keep.shape[0],),
        in_specs=[block, block],
        out_specs=block,
        out_shape=jax.ShapeDtypeStruct(keep.shape, BF16),
        cost_estimate=pl.CostEstimate(flops=1, bytes_accessed=1, transcendentals=0),
        name="pair_sum",
    )(keep, got)


def folded(array, *lead):
    return array.reshape(lead + (-1, 128))


def ring_sum(chunks, axis):
    size = lax.axis_size(axis)
    me = lax.axis_index(axis).astype(jnp.uint32)

    def chunk(by):
        at = lax.bitwise_and(me + jnp.uint32(by), jnp.uint32(size - 1))
        return lax.dynamic_index_in_dim(chunks, at, 0, keepdims=False)

    total = chunk(0).astype(F32)
    for by in range(1, size):
        moved = lax.ppermute(chunk(by), axis, [(i, (i + by) % size) for i in range(size)])
        total = total + moved.astype(F32)
    return total


def summed_by_frame(part):
    z, xhi = lax.axis_size("z"), lax.axis_size("xhi")
    after_z = ring_sum(folded(part, z, xhi), "z").astype(BF16)
    return ring_sum(after_z, "xhi")


def summed_at_once(mine):
    rest = ("xlo", "y", "z", "xhi")
    count = lax.axis_size(rest)
    arrived = lax.all_to_all(folded(mine, count), rest, 0, 0, tiled=False)
    return jnp.sum(arrived.astype(F32), axis=0)


def shifted(shard, by):
    size = lax.axis_size(TILE)
    return lax.ppermute(shard, TILE, [(i, (i + by) % size) for i in range(size)])


def own_rows(weight):
    count = lax.axis_size(TILE + FRAME)
    per_device = weight.shape[0] // count
    at = lax.axis_index(TILE + FRAME) * per_device
    return lax.dynamic_slice_in_dim(weight, at, per_device, axis=0).astype(F32)


def finished(total, qkv, gain, tokens):
    features, wide = qkv.shape
    summed = total.reshape(-1, wide + features) * (1.0 / math.sqrt(tokens))
    d_qkv = summed[:, :wide]
    d_gain = jnp.sum(own_rows(qkv) * d_qkv, axis=1) / own_rows(gain)
    return d_gain, d_qkv, summed[:, wide:]


def shards(tokens, gain_space, qkv_space, out_space, gain_time, qkv_time, out_time, cotangent):
    frames, lat, width, features = tokens.shape
    total = frames * lat * width * lax.axis_size(TILE) * lax.axis_size(FRAME)
    gain_s = gain_space.reshape(1, features)
    gain_t = gain_time.reshape(1, features)
    core = lax.axis_index("core").astype(jnp.int32).reshape(1)
    tiles = lax.axis_size(("xlo", "y"))

    peers = lax.axis_size(FRAME)

    def exchanged(chunks):
        return lax.all_to_all(chunks, FRAME, 0, 0, tiled=False)

    west = shifted(tokens, 1)
    east = shifted(tokens, -1)
    cot_chunks = cotangent.reshape(frames, peers, lat // peers, width, features)
    cot_rows = exchanged(cot_chunks.transpose(1, 0, 2, 3, 4))
    y_s, q_s, kv_s, p_s, o_s, mid = spatial_forward(
        tokens, west, east, gain_s, qkv_space, out_space, peers
    )
    both_rows, left_t, right_t = temporal(exchanged(mid), cot_rows, gain_t, qkv_time, out_time)
    both = exchanged(both_rows)
    keep_t, send_t = term_time(core, left_t, right_t, tiles)
    mine_t = paired(keep_t, send_t)
    dproj = back_projection(both, out_space, frames)
    dproj, mine_t = lax.optimization_barrier((dproj, mine_t))
    arrived_t = lax.all_to_all(mine_t, ("xlo", "y"), 0, 0, tiled=False)
    dq, dkv, own, for_west, for_east = spatial_backward(dproj, qkv_space, q_s, kv_s, p_s, lat)
    from_east = shifted(for_west, -1)
    from_west = shifted(for_east, 1)
    keep_s, send_s = term_space(core, y_s, dq, dkv, o_s, both, tiles)
    send_s, arrived_t, from_east, from_west = lax.optimization_barrier(
        (send_s, arrived_t, from_east, from_west)
    )
    mine_s = paired(keep_s, send_s)
    summed_space = summed_at_once(mine_s)
    part_t = jnp.sum(arrived_t.astype(F32), axis=0).astype(BF16)
    summed_time = summed_by_frame(part_t)
    layer_out = both[:, frames:].transpose(1, 0, 2, 3, 4).reshape(tokens.shape)
    grad_tokens = final_norm(tokens, gain_s, both, own, from_east, from_west)
    return (
        (layer_out, grad_tokens)
        + finished(summed_space, qkv_space, gain_space, total)
        + finished(summed_time, qkv_time, gain_time, total)
    )


def solution(mesh):
    fine = Mesh(mesh.devices.reshape(2, 4, 2, 4, 2), TILE + FRAME)
    token_spec = P(FRAME, None, TILE, None)
    row_spec = P(TILE + FRAME)
    return jax.shard_map(
        shards,
        mesh=fine,
        in_specs=(token_spec, P(), P(), P(), P(), P(), P(), token_spec),
        out_specs=(token_spec, token_spec) + (row_spec,) * 6,
        check_vma=False,
    )
```

```python
import functools
import math

import jax
import jax.numpy as jnp
from jax import lax
from jax.experimental import pallas as pl
from jax.experimental.pallas import tpu as pltpu
from jax.sharding import Mesh
from jax.sharding import PartitionSpec as P

HDIM = 64
BH = 8
LANES = 4 * HDIM
EPS = 1e-05
F32 = jnp.float32
BF16 = jnp.bfloat16
TILE = ("xlo", "y", "core")
FRAME = ("z", "xhi")
VMEM_LIMIT = 56 * 1024 * 1024


def dot(left, right, left_dim=1, right_dim=0):
    return lax.dot_general(
        left, right, (((left_dim,), (right_dim,)), ((), ())), preferred_element_type=F32
    )


def normalized(rows):
    centred = rows - jnp.mean(rows, axis=-1, keepdims=True)
    variance = jnp.mean(centred * centred, axis=-1, keepdims=True)
    inverse = lax.rsqrt(variance + EPS)
    return centred * inverse, inverse


def norm_back(unit, inverse, gain, d_out):
    d_unit = d_out * gain
    along = jnp.mean(d_unit * unit, axis=-1, keepdims=True)
    return inverse * (d_unit - jnp.mean(d_unit, axis=-1, keepdims=True) - unit * along)


def head_mask(rows):
    row_head = lax.broadcasted_iota(jnp.int32, (4 * rows, LANES), 0) // rows
    lane_head = lax.broadcasted_iota(jnp.int32, (4 * rows, LANES), 1) // HDIM
    return row_head == lane_head


def spread(group, mask):
    stacked = jnp.concatenate([group] * 4, axis=0)
    return jnp.where(mask, stacked, jnp.zeros_like(stacked))


def gathered(wide, rows):
    lane_head = lax.broadcasted_iota(jnp.int32, (rows, LANES), 1) // HDIM
    parts = [wide[h * rows : (h + 1) * rows] for h in range(4)]
    low = jnp.where(lane_head == 0, parts[0], parts[1])
    high = jnp.where(lane_head == 2, parts[2], parts[3])
    return jnp.where(lane_head < 2, low, high)


def softmax_rows(scores):
    top = jnp.max(scores, axis=0, keepdims=True)
    exponent = jnp.exp(scores - top)
    return exponent * (1.0 / jnp.sum(exponent, axis=0, keepdims=True))


def key_ranges(blocks, step):
    return [(max(b - 1, 0) * step, min(b + 2, blocks) * step) for b in range(blocks)]


def spatial_forward_kernel(
    own_ref, west_ref, east_ref, gain_ref, qkv_ref, out_ref,
    y_ref, q_ref, kv_ref, p_ref, o_ref, mid_ref,
):
    _, lat, width, features = own_ref.shape
    rows = BH * width
    blocks = lat // BH
    step = 3 * rows
    gain = gain_ref[...]
    for tile, ref in enumerate((west_ref, own_ref, east_ref)):
        wide = ref[0].astype(F32).reshape(lat * width, features)
        unit, _ = normalized(wide)
        y = (unit * gain).astype(BF16)
        for b in range(blocks):
            at = b * step + tile * rows
            y_ref[0, at : at + rows] = y[b * rows : (b + 1) * rows]
        if tile == 1:
            q_ref[0] = (dot(y, qkv_ref[:, :features]).astype(BF16) * HDIM ** (-0.5)).astype(BF16)
    for b in range(blocks):
        part = slice(b * step, (b + 1) * step)
        kv_ref[0, part] = dot(y_ref[0, part], qkv_ref[:, features:]).astype(BF16)
    mask = head_mask(rows)
    offset = 0
    for b, (low, high) in enumerate(key_ranges(blocks, step)):
        span = high - low
        for g in range(features // LANES):
            lanes = slice(g * LANES, (g + 1) * LANES)
            queries = spread(q_ref[0, b * rows : (b + 1) * rows, lanes], mask)
            keys = kv_ref[0, low:high, lanes]
            values = kv_ref[0, low:high, features + g * LANES : features + (g + 1) * LANES]
            weights = softmax_rows(dot(keys, queries, 1, 1)).astype(BF16)
            p_ref[0, g, offset : offset + span] = weights
            mixed = dot(weights, values, 0, 0)
            o_ref[0, b * rows : (b + 1) * rows, lanes] = gathered(mixed, rows).astype(BF16)
        offset += span
    wide = own_ref[0].astype(F32).reshape(lat * width, features)
    mid = wide + dot(o_ref[0], out_ref[...])
    mid_ref[:, 0] = mid.reshape(-1, mid_ref.shape[2], width, features).astype(BF16)


def full(shape):
    return pl.BlockSpec(shape, lambda *_: (0,) * len(shape))


def per_step(shape):
    return pl.BlockSpec((1,) + shape, lambda i: (i,) + (0,) * len(shape))


def cost(microseconds):
    return pl.CostEstimate(
        flops=microseconds * 10**9, bytes_accessed=4 << 20, transcendentals=2 * 10**6
    )


def grouped(peers, lat, width, features):
    return pl.BlockSpec((peers, 1, lat // peers, width, features), lambda i: (0, i, 0, 0, 0))


def spatial_forward(own, west, east, gain, qkv, out, peers):
    frames, lat, width, features = own.shape
    rows = lat * width
    blocks = lat // BH
    spans = sum(h - l for l, h in key_ranges(blocks, 3 * BH * width))
    groups = features // LANES
    outs = (
        ((3 * rows, features), BF16),
        ((rows, features), BF16),
        ((3 * rows, 2 * features), BF16),
        ((groups, spans, LANES), BF16),
        ((rows, features), BF16),
    )
    mid_shape = (peers, frames, lat // peers, width, features)
    return pl.pallas_call(
        spatial_forward_kernel,
        grid=(frames,),
        in_specs=[per_step((lat, width, features))] * 3
        + [full((1, features)), full(qkv.shape), full(out.shape)],
        out_specs=[per_step(shape) for shape, _ in outs] + [grouped(peers, lat, width, features)],
        out_shape=[jax.ShapeDtypeStruct((frames,) + shape, kind) for shape, kind in outs]
        + [jax.ShapeDtypeStruct(mid_shape, BF16)],
        compiler_params=pltpu.CompilerParams(vmem_limit_bytes=VMEM_LIMIT),
        cost_estimate=cost(14),
        name="spatial_forward",
    )(own, west, east, gain, qkv, out)


def temporal_kernel(
    mid_ref, cot_ref, gain_ref, qkv_ref, out_ref,
    both_ref, left_ref, right_ref,
    packed_ref, dproj_ref,
):
    peers, frames, lat, width, features = mid_ref.shape
    rows = peers * frames * width
    gain = gain_ref[...]
    scale = HDIM ** (-0.5)

    def by_row(ref, row):
        return ref[:, :, row].astype(F32).reshape(rows, features)

    for row in range(lat):
        part = slice(row * rows, (row + 1) * rows)
        unit, _ = normalized(by_row(mid_ref, row))
        left_ref[part, :features] = (unit * gain).astype(BF16)
        right_ref[part, 3 * features :] = by_row(cot_ref, row).astype(BF16)
    packed_ref[...] = dot(left_ref[:, :features], qkv_ref[...]).astype(BF16)
    dproj_ref[...] = dot(right_ref[:, 3 * features :], out_ref[...], 1, 1).astype(BF16)
    mask = head_mask(rows)
    key_col = lax.broadcasted_iota(jnp.int32, (rows, 4 * rows), 0) % width
    query_col = lax.broadcasted_iota(jnp.int32, (rows, 4 * rows), 1) % width
    same = key_col == query_col
    for row in range(lat):
        part = slice(row * rows, (row + 1) * rows)
        for g in range(features // LANES):
            lanes = [
                slice(s * features + g * LANES, s * features + (g + 1) * LANES) for s in range(3)
            ]
            queries = spread((packed_ref[part, lanes[0]] * scale).astype(BF16), mask)
            keys = packed_ref[part, lanes[1]]
            values = packed_ref[part, lanes[2]]
            scores = jnp.where(same, dot(keys, queries, 1, 1), -1e30)
            wide = softmax_rows(scores)
            weights = wide.astype(BF16)
            mixed = dot(weights, values, 0, 0)
            left_ref[part, lanes[1]] = gathered(mixed, rows).astype(BF16)
            d_out = spread(dproj_ref[part, lanes[0]], mask)
            d_weights = dot(values, d_out, 1, 1)
            delta = jnp.sum(wide * d_weights, axis=0, keepdims=True)
            d_scores = (wide * (d_weights - delta)).astype(BF16)
            d_query = gathered(dot(d_scores, keys, 0, 0), rows) * scale
            right_ref[part, lanes[0]] = d_query.astype(BF16)
            right_ref[part, lanes[1]] = dot(d_scores, queries).astype(BF16)
            right_ref[part, lanes[2]] = dot(weights, d_out).astype(BF16)
    layer = dot(left_ref[:, features:], out_ref[...])
    d_y = dot(right_ref[:, : 3 * features], qkv_ref[...], 1, 1)
    shape = (peers, frames, width, features)
    for row in range(lat):
        part = slice(row * rows, (row + 1) * rows)
        mid = by_row(mid_ref, row)
        unit, inverse = normalized(mid)
        d_mid = by_row(cot_ref, row) + norm_back(unit, inverse, gain, d_y[part])
        both_ref[:, :frames, row] = d_mid.reshape(shape).astype(BF16)
        both_ref[:, frames:, row] = (mid + layer[part]).reshape(shape).astype(BF16)


def temporal(mid, cot, gain, qkv, out):
    peers, frames, lat, width, features = mid.shape
    rows = peers * frames * lat * width
    return pl.pallas_call(
        temporal_kernel,
        out_shape=[
            jax.ShapeDtypeStruct((peers, 2 * frames, lat, width, features), BF16),
            jax.ShapeDtypeStruct((rows, 2 * features), BF16),
            jax.ShapeDtypeStruct((rows, 4 * features), BF16),
        ],
        scratch_shapes=[
            pltpu.VMEM((rows, 3 * features), BF16),
            pltpu.VMEM((rows, features), BF16),
        ],
        compiler_params=pltpu.CompilerParams(vmem_limit_bytes=VMEM_LIMIT),
        cost_estimate=cost(18),
        name="temporal",
    )(mid, cot, gain, qkv, out)


def back_projection_kernel(dmid_ref, out_ref, dproj_ref):
    rows, features = dproj_ref.shape[1:]
    dmid = dmid_ref[...].astype(F32).reshape(rows, features).astype(BF16)
    dproj_ref[0] = dot(dmid, out_ref[...], 1, 1).astype(BF16)


def back_projection(dmid, out, frames):
    peers, _, each, width, features = dmid.shape
    rows = peers * each * width
    return pl.pallas_call(
        back_projection_kernel,
        grid=(frames,),
        in_specs=[grouped(peers, peers * each, width, features), full(out.shape)],
        out_specs=per_step((rows, features)),
        out_shape=jax.ShapeDtypeStruct((frames, rows, features), BF16),
        compiler_params=pltpu.CompilerParams(vmem_limit_bytes=VMEM_LIMIT),
        cost_estimate=cost(30),
        name="back_projection",
    )(dmid, out)


def spatial_backward_kernel(
    dproj_ref, qkv_ref, q_ref, kv_ref, p_ref,
    dq_ref, dkv_ref, own_ref, west_ref, east_ref,
    acc_ref,
):
    _, lat, width, features = own_ref.shape
    rows = BH * width
    blocks = lat // BH
    step = 3 * rows
    mask = head_mask(rows)
    acc_ref[...] = jnp.zeros_like(acc_ref)
    offset = 0
    for b, (low, high) in enumerate(key_ranges(blocks, step)):
        span = high - low
        block = slice(b * rows, (b + 1) * rows)
        for g in range(features // LANES):
            lanes = slice(g * LANES, (g + 1) * LANES)
            late = slice(features + g * LANES, features + (g + 1) * LANES)
            queries = spread(q_ref[0, block, lanes], mask)
            d_out = spread(dproj_ref[0, block, lanes], mask)
            keys = kv_ref[0, low:high, lanes]
            values = kv_ref[0, low:high, late]
            weights = p_ref[0, g, offset : offset + span]
            wide = weights.astype(F32)
            d_weights = dot(values, d_out, 1, 1)
            delta = jnp.sum(wide * d_weights, axis=0, keepdims=True)
            d_scores = (wide * (d_weights - delta)).astype(BF16)
            d_query = gathered(dot(d_scores, keys, 0, 0), rows) * HDIM ** (-0.5)
            dq_ref[0, block, lanes] = d_query.astype(BF16)
            acc_ref[low:high, lanes] += dot(d_scores, queries)
            acc_ref[low:high, late] += dot(weights, d_out)
        offset += span
    dkv_ref[0] = acc_ref[...].astype(BF16)
    for b in range(blocks):
        part = slice(b * step, (b + 1) * step)
        d_y = dot(dkv_ref[0, part], qkv_ref[:, features:], 1, 1)
        block = slice(b * rows, (b + 1) * rows)
        d_own = d_y[rows : 2 * rows] + dot(dq_ref[0, block], qkv_ref[:, :features], 1, 1)
        for ref, value in ((west_ref, d_y[:rows]), (own_ref, d_own), (east_ref, d_y[2 * rows :])):
            ref[0, b * BH : (b + 1) * BH] = value.reshape(BH, width, features).astype(BF16)


def spatial_backward(dproj, qkv, q, kv, p, lat):
    frames, rows, features = dproj.shape
    width = rows // lat
    outs = (
        (rows, features),
        (3 * rows, 2 * features),
        (lat, width, features),
        (lat, width, features),
        (lat, width, features),
    )
    return pl.pallas_call(
        spatial_backward_kernel,
        grid=(frames,),
        in_specs=[
            per_step((rows, features)),
            full(qkv.shape),
            per_step(q.shape[1:]),
            per_step(kv.shape[1:]),
            per_step(p.shape[1:]),
        ],
        out_specs=[per_step(shape) for shape in outs],
        out_shape=[jax.ShapeDtypeStruct((frames,) + shape, BF16) for shape in outs],
        scratch_shapes=[
            pltpu.VMEM((3 * rows, 2 * features), F32),
        ],
        compiler_params=pltpu.CompilerParams(vmem_limit_bytes=VMEM_LIMIT),
        cost_estimate=cost(20),
        name="spatial_backward",
    )(dproj, qkv, q, kv, p)


def final_kernel(tokens_ref, gain_ref, dmid_ref, own_ref, first_ref, second_ref, grad_ref):
    _, lat, width, features = tokens_ref.shape

    def flat(ref):
        return ref[0].astype(F32).reshape(lat * width, features)

    unit, inverse = normalized(flat(tokens_ref))
    d_y = flat(own_ref) + flat(first_ref) + flat(second_ref)
    d_mid = dmid_ref[...].astype(F32).reshape(lat * width, features)
    grad = d_mid + norm_back(unit, inverse, gain_ref[...], d_y)
    grad_ref[0] = grad.reshape(lat, width, features)


def final_norm(tokens, gain, dmid, own, first, second):
    frames, lat, width, features = tokens.shape
    block = per_step((lat, width, features))
    return pl.pallas_call(
        final_kernel,
        grid=(frames,),
        in_specs=[block, full((1, features)), grouped(dmid.shape[0], lat, width, features)]
        + [block] * 3,
        out_specs=block,
        out_shape=jax.ShapeDtypeStruct(tokens.shape, F32),
        compiler_params=pltpu.CompilerParams(vmem_limit_bytes=VMEM_LIMIT),
        cost_estimate=cost(3),
        name="final_norm",
    )(tokens, gain, dmid, own, first, second)


def split_store(core_ref, term, keep_ref, send_ref):
    tiles, rows, columns = keep_ref.shape
    pairs = term.reshape(tiles, 2, rows, columns)
    first = core_ref[0] == 0
    for tile in range(tiles):
        even, odd = pairs[tile, 0], pairs[tile, 1]
        keep_ref[tile] = jnp.where(first, even, odd).astype(BF16)
        send_ref[tile] = jnp.where(first, odd, even).astype(BF16)


def term_time_kernel(core_ref, left_ref, right_ref, keep_ref, send_ref):
    split_store(core_ref, dot(left_ref[...], right_ref[...], 0, 0), keep_ref, send_ref)


def split_call(kernel, core, operands, specs, features, tiles, name, flops):
    shape = (tiles, features // (2 * tiles), 4 * features)
    block = pl.BlockSpec(shape[:2] + (features,), lambda i, core: (0, 0, i))
    return pl.pallas_call(
        kernel,
        grid_spec=pltpu.PrefetchScalarGridSpec(
            num_scalar_prefetch=1, grid=(4,), in_specs=specs, out_specs=[block, block]
        ),
        out_shape=[jax.ShapeDtypeStruct(shape, BF16)] * 2,
        compiler_params=pltpu.CompilerParams(vmem_limit_bytes=VMEM_LIMIT),
        cost_estimate=pl.CostEstimate(flops=flops, bytes_accessed=1, transcendentals=0),
        name=name,
    )(core, *operands)


def term_time(core, left, right, tiles):
    rows, double = left.shape
    features = double // 2
    specs = [
        pl.BlockSpec((rows, features), lambda i, core: (0, i // 3)),
        pl.BlockSpec((rows, features), lambda i, core: (0, i)),
    ]
    return split_call(
        term_time_kernel, core, (left, right), specs, features, tiles,
        "term_time", 1,
    )


def term_space_kernel(core_ref, y_ref, dq_ref, dkv_ref, o_ref, dmid_ref, keep_ref, send_ref):
    step = pl.program_id(0)
    frames, ext, features = y_ref.shape
    own = dq_ref.shape[1]

    @pl.when(step == 0)
    def _():
        part = BH * dmid_ref.shape[3]
        blocks = own // part
        pieces = [
            y_ref[f, (3 * b + 1) * part : (3 * b + 2) * part]
            for f in range(frames)
            for b in range(blocks)
        ]
        left = jnp.concatenate(pieces, axis=0)
        right = dq_ref[...].reshape(frames * own, features)
        split_store(core_ref, dot(left, right, 0, 0), keep_ref, send_ref)

    @pl.when((step == 1) | (step == 2))
    def _():
        left = y_ref[...].reshape(frames * ext, features)
        right = dkv_ref[...].reshape(frames * ext, features)
        split_store(core_ref, dot(left, right, 0, 0), keep_ref, send_ref)

    @pl.when(step == 3)
    def _():
        left = o_ref[...].reshape(frames * own, features)
        right = [dmid_ref[:, f].astype(F32).reshape(own, features) for f in range(frames)]
        right = jnp.concatenate(right, axis=0).astype(BF16)
        split_store(core_ref, dot(left, right, 0, 0), keep_ref, send_ref)


def term_space(core, y, dq, dkv, o, dmid, tiles):
    features = y.shape[-1]

    def whole(array):
        return pl.BlockSpec(array.shape, lambda i, core: (0,) * array.ndim)

    specs = [
        whole(y),
        whole(dq),
        pl.BlockSpec(dkv.shape[:2] + (features,), lambda i, core: (0, 0, jnp.clip(i - 1, 0, 1))),
        whole(o),
        pl.BlockSpec(
            (dmid.shape[0], y.shape[0]) + dmid.shape[2:], lambda i, core: (0,) * dmid.ndim
        ),
    ]
    return split_call(
        term_space_kernel, core, (y, dq, dkv, o, dmid), specs, features, tiles, "term_space", 1,
    )


def pair_fold_kernel(peers, keep_ref, got_ref, sum_ref, row_ref):
    tiles, rows, columns = keep_ref.shape
    across = columns // 128
    each = rows // peers
    for tile in range(tiles):
        total = keep_ref[tile].astype(F32) + got_ref[tile].astype(F32)
        base = tile * across * rows
        for c in range(across):
            at = base + c * rows
            row_ref[at : at + rows] = total[:, c * 128 : (c + 1) * 128]
        for peer in range(peers):
            for r in range(0, each, 2):
                start = base + peer * each + r
                pair = [row_ref[pl.ds(start + k, across, stride=rows)] for k in range(2)]
                at = r * across
                sum_ref[tile * peers + peer, at : at + 2 * across] = jnp.concatenate(
                    pair, axis=0
                ).astype(BF16)


def paired(keep, send, peers):
    got = lax.ppermute(send, "core", [(0, 1), (1, 0)])
    tiles, rows, columns = keep.shape
    at_once = tiles // 4
    height = rows // peers * columns // 128
    block = pl.BlockSpec((at_once, rows, columns), lambda i: (i, 0, 0))
    return pl.pallas_call(
        functools.partial(pair_fold_kernel, peers),
        grid=(4,),
        in_specs=[block, block],
        out_specs=pl.BlockSpec((at_once * peers, height, 128), lambda i: (i, 0, 0)),
        out_shape=jax.ShapeDtypeStruct((tiles * peers, height, 128), BF16),
        scratch_shapes=[pltpu.VMEM((at_once * columns // 128 * rows, 128), F32)],
        compiler_params=pltpu.CompilerParams(vmem_limit_bytes=16 << 20),
        cost_estimate=pl.CostEstimate(flops=1, bytes_accessed=1, transcendentals=0),
        name="pair_fold",
    )(keep, got)


def spread_out(mine):
    return lax.all_to_all(mine, ("xlo", "y", "z", "xhi"), 0, 0, tiled=False)


def shifted(shard, by):
    size = lax.axis_size(TILE)
    return lax.ppermute(shard, TILE, [(i, (i + by) % size) for i in range(size)])


def own_rows(weight):
    count = lax.axis_size(TILE + FRAME)
    per_device = weight.shape[0] // count
    at = lax.axis_index(TILE + FRAME) * per_device
    return lax.dynamic_slice_in_dim(weight, at, per_device, axis=0).astype(F32)


def finished(arrived, qkv, gain, tokens):
    features, wide = qkv.shape
    total = jnp.sum(arrived.astype(F32), axis=0)
    summed = total.reshape(-1, wide + features) * (1.0 / math.sqrt(tokens))
    d_qkv = summed[:, :wide]
    d_gain = jnp.sum(own_rows(qkv) * d_qkv, axis=1) / own_rows(gain)
    return d_gain, d_qkv, summed[:, wide:]


def shards(tokens, gain_space, qkv_space, out_space, gain_time, qkv_time, out_time, cotangent):
    frames, lat, width, features = tokens.shape
    total = frames * lat * width * lax.axis_size(TILE) * lax.axis_size(FRAME)
    gain_s = gain_space.reshape(1, features)
    gain_t = gain_time.reshape(1, features)
    core = lax.axis_index("core").astype(jnp.int32).reshape(1)
    tiles = lax.axis_size(("xlo", "y"))

    peers = lax.axis_size(FRAME)

    def exchanged(chunks):
        return lax.all_to_all(chunks, FRAME, 0, 0, tiled=False)

    west = shifted(tokens, 1)
    east = shifted(tokens, -1)
    cot_chunks = cotangent.reshape(frames, peers, lat // peers, width, features)
    cot_rows = exchanged(cot_chunks.transpose(1, 0, 2, 3, 4))
    y_s, q_s, kv_s, p_s, o_s, mid = spatial_forward(
        tokens, west, east, gain_s, qkv_space, out_space, peers
    )
    both_rows, left_t, right_t = temporal(exchanged(mid), cot_rows, gain_t, qkv_time, out_time)
    both = exchanged(both_rows)
    keep_t, send_t = term_time(core, left_t, right_t, tiles)
    mine_t = paired(keep_t, send_t, peers)
    dproj = back_projection(both, out_space, frames)
    dproj, mine_t = lax.optimization_barrier((dproj, mine_t))
    arrived_t = spread_out(mine_t)
    dq, dkv, own, for_west, for_east = spatial_backward(dproj, qkv_space, q_s, kv_s, p_s, lat)
    from_east = shifted(for_west, -1)
    from_west = shifted(for_east, 1)
    keep_s, send_s = term_space(core, y_s, dq, dkv, o_s, both, tiles)
    send_s, arrived_t, from_east, from_west = lax.optimization_barrier(
        (send_s, arrived_t, from_east, from_west)
    )
    arrived_s = spread_out(paired(keep_s, send_s, peers))
    layer_out = both[:, frames:].transpose(1, 0, 2, 3, 4).reshape(tokens.shape)
    grad_tokens = final_norm(tokens, gain_s, both, own, from_east, from_west)
    return (
        (layer_out, grad_tokens)
        + finished(arrived_s, qkv_space, gain_space, total)
        + finished(arrived_t, qkv_time, gain_time, total)
    )


def solution(mesh):
    fine = Mesh(mesh.devices.reshape(2, 4, 2, 4, 2), TILE + FRAME)
    token_spec = P(FRAME, None, TILE, None)
    row_spec = P(TILE + FRAME)
    return jax.shard_map(
        shards,
        mesh=fine,
        in_specs=(token_spec, P(), P(), P(), P(), P(), P(), token_spec),
        out_specs=(token_spec, token_spec) + (row_spec,) * 6,
        check_vma=False,
    )
```

```python
import functools
import math

import jax
import jax.numpy as jnp
from jax import lax
from jax.experimental import pallas as pl
from jax.experimental.pallas import tpu as pltpu
from jax.sharding import Mesh
from jax.sharding import PartitionSpec as P

HDIM = 64
BH = 8
LANES = 4 * HDIM
EPS = 1e-05
F32 = jnp.float32
BF16 = jnp.bfloat16
TILE = ("xlo", "y", "core")
FRAME = ("z", "xhi")


def dot(left, right, left_dim=1, right_dim=0):
    return lax.dot_general(
        left, right, (((left_dim,), (right_dim,)), ((), ())), preferred_element_type=F32
    )


def normalized(rows):
    centred = rows - jnp.mean(rows, axis=-1, keepdims=True)
    variance = jnp.mean(centred * centred, axis=-1, keepdims=True)
    inverse = lax.rsqrt(variance + EPS)
    return centred * inverse, inverse


def norm_back(unit, inverse, gain, d_out):
    d_unit = d_out * gain
    along = jnp.mean(d_unit * unit, axis=-1, keepdims=True)
    return inverse * (d_unit - jnp.mean(d_unit, axis=-1, keepdims=True) - unit * along)


def head_mask(rows):
    row_head = lax.broadcasted_iota(jnp.int32, (4 * rows, LANES), 0) // rows
    lane_head = lax.broadcasted_iota(jnp.int32, (4 * rows, LANES), 1) // HDIM
    return row_head == lane_head


def spread(group, mask):
    stacked = jnp.concatenate([group] * 4, axis=0)
    return jnp.where(mask, stacked, jnp.zeros_like(stacked))


def gathered(wide, rows):
    lane_head = lax.broadcasted_iota(jnp.int32, (rows, LANES), 1) // HDIM
    parts = [wide[h * rows : (h + 1) * rows] for h in range(4)]
    low = jnp.where(lane_head == 0, parts[0], parts[1])
    high = jnp.where(lane_head == 2, parts[2], parts[3])
    return jnp.where(lane_head < 2, low, high)


def softmax_rows(scores):
    top = jnp.max(scores, axis=0, keepdims=True)
    exponent = jnp.exp(scores - top)
    return exponent * (1.0 / jnp.sum(exponent, axis=0, keepdims=True))


def key_ranges(blocks, step):
    return [(max(b - 1, 0) * step, min(b + 2, blocks) * step) for b in range(blocks)]


def spatial_forward_kernel(
    own_ref, west_ref, east_ref, gain_ref, qkv_ref, out_ref,
    y_ref, q_ref, kv_ref, p_ref, o_ref, mid_ref,
):
    _, lat, width, features = own_ref.shape
    rows = BH * width
    blocks = lat // BH
    step = 3 * rows
    gain = gain_ref[...]
    for tile, ref in enumerate((west_ref, own_ref, east_ref)):
        wide = ref[0].astype(F32).reshape(lat * width, features)
        unit, _ = normalized(wide)
        y = (unit * gain).astype(BF16)
        for b in range(blocks):
            at = b * step + tile * rows
            y_ref[0, at : at + rows] = y[b * rows : (b + 1) * rows]
        if tile == 1:
            q_ref[0] = (dot(y, qkv_ref[:, :features]).astype(BF16) * HDIM ** (-0.5)).astype(BF16)
    for b in range(blocks):
        part = slice(b * step, (b + 1) * step)
        kv_ref[0, part] = dot(y_ref[0, part], qkv_ref[:, features:]).astype(BF16)
    mask = head_mask(rows)
    offset = 0
    for b, (low, high) in enumerate(key_ranges(blocks, step)):
        span = high - low
        for g in range(features // LANES):
            lanes = slice(g * LANES, (g + 1) * LANES)
            queries = spread(q_ref[0, b * rows : (b + 1) * rows, lanes], mask)
            keys = kv_ref[0, low:high, lanes]
            values = kv_ref[0, low:high, features + g * LANES : features + (g + 1) * LANES]
            weights = softmax_rows(dot(keys, queries, 1, 1)).astype(BF16)
            p_ref[0, g, offset : offset + span] = weights
            mixed = dot(weights, values, 0, 0)
            o_ref[0, b * rows : (b + 1) * rows, lanes] = gathered(mixed, rows).astype(BF16)
        offset += span
    wide = own_ref[0].astype(F32).reshape(lat * width, features)
    mid = wide + dot(o_ref[0], out_ref[...])
    mid_ref[:, 0] = mid.reshape(-1, mid_ref.shape[2], width, features).astype(BF16)


def full(shape):
    return pl.BlockSpec(shape, lambda *_: (0,) * len(shape), pipeline_mode=pl.Buffered(1))


def per_step(shape):
    return pl.BlockSpec((1,) + shape, lambda i: (i,) + (0,) * len(shape))


def cost(microseconds):
    return pl.CostEstimate(
        flops=microseconds * 10**9, bytes_accessed=4 << 20, transcendentals=2 * 10**6
    )


def grouped(peers, lat, width, features):
    return pl.BlockSpec((peers, 1, lat // peers, width, features), lambda i: (0, i, 0, 0, 0))


def spatial_forward(own, west, east, gain, qkv, out, peers):
    frames, lat, width, features = own.shape
    rows = lat * width
    blocks = lat // BH
    spans = sum(h - l for l, h in key_ranges(blocks, 3 * BH * width))
    groups = features // LANES
    outs = (
        ((3 * rows, features), BF16),
        ((rows, features), BF16),
        ((3 * rows, 2 * features), BF16),
        ((groups, spans, LANES), BF16),
        ((rows, features), BF16),
    )
    mid_shape = (peers, frames, lat // peers, width, features)
    return pl.pallas_call(
        spatial_forward_kernel,
        grid=(frames,),
        in_specs=[per_step((lat, width, features))] * 3
        + [full((1, features)), full(qkv.shape), full(out.shape)],
        out_specs=[per_step(shape) for shape, _ in outs] + [grouped(peers, lat, width, features)],
        out_shape=[pltpu.HBM((frames,) + shape, kind) for shape, kind in outs]
        + [pltpu.HBM(mid_shape, BF16)],
        compiler_params=pltpu.CompilerParams(vmem_limit_bytes=36 << 20),
        cost_estimate=cost(14),
        name="spatial_forward",
    )(*[from_hbm(a) for a in (own, west, east)], gain, from_hbm(qkv), from_hbm(out))


def temporal_kernel(
    mid_ref, cot_ref, gain_ref, qkv_ref, out_ref,
    both_ref, left_ref, right_ref,
    packed_ref, dproj_ref,
):
    peers, frames, lat, width, features = mid_ref.shape
    rows = peers * frames * width
    gain = gain_ref[...]
    scale = HDIM ** (-0.5)

    def by_row(ref, row):
        return ref[:, :, row].astype(F32).reshape(rows, features)

    for row in range(lat):
        part = slice(row * rows, (row + 1) * rows)
        unit, _ = normalized(by_row(mid_ref, row))
        left_ref[part, :features] = (unit * gain).astype(BF16)
        right_ref[part, 3 * features :] = by_row(cot_ref, row).astype(BF16)
    packed_ref[...] = dot(left_ref[:, :features], qkv_ref[...]).astype(BF16)
    dproj_ref[...] = dot(right_ref[:, 3 * features :], out_ref[...], 1, 1).astype(BF16)
    mask = head_mask(rows)
    key_col = lax.broadcasted_iota(jnp.int32, (rows, 4 * rows), 0) % width
    query_col = lax.broadcasted_iota(jnp.int32, (rows, 4 * rows), 1) % width
    same = key_col == query_col
    for row in range(lat):
        part = slice(row * rows, (row + 1) * rows)
        for g in range(features // LANES):
            lanes = [
                slice(s * features + g * LANES, s * features + (g + 1) * LANES) for s in range(3)
            ]
            queries = spread((packed_ref[part, lanes[0]] * scale).astype(BF16), mask)
            keys = packed_ref[part, lanes[1]]
            values = packed_ref[part, lanes[2]]
            scores = jnp.where(same, dot(keys, queries, 1, 1), -1e30)
            wide = softmax_rows(scores)
            weights = wide.astype(BF16)
            mixed = dot(weights, values, 0, 0)
            left_ref[part, lanes[1]] = gathered(mixed, rows).astype(BF16)
            d_out = spread(dproj_ref[part, lanes[0]], mask)
            d_weights = dot(values, d_out, 1, 1)
            delta = jnp.sum(wide * d_weights, axis=0, keepdims=True)
            d_scores = (wide * (d_weights - delta)).astype(BF16)
            d_query = gathered(dot(d_scores, keys, 0, 0), rows) * scale
            right_ref[part, lanes[0]] = d_query.astype(BF16)
            right_ref[part, lanes[1]] = dot(d_scores, queries).astype(BF16)
            right_ref[part, lanes[2]] = dot(weights, d_out).astype(BF16)
    layer = dot(left_ref[:, features:], out_ref[...])
    d_y = dot(right_ref[:, : 3 * features], qkv_ref[...], 1, 1)
    shape = (peers, frames, width, features)
    for row in range(lat):
        part = slice(row * rows, (row + 1) * rows)
        mid = by_row(mid_ref, row)
        unit, inverse = normalized(mid)
        d_mid = by_row(cot_ref, row) + norm_back(unit, inverse, gain, d_y[part])
        both_ref[:, :frames, row] = d_mid.reshape(shape).astype(BF16)
        both_ref[:, frames:, row] = (mid + layer[part]).reshape(shape).astype(BF16)


def temporal(mid, cot, gain, qkv, out):
    peers, frames, lat, width, features = mid.shape
    rows = peers * frames * lat * width
    return pl.pallas_call(
        temporal_kernel,
        out_shape=[
            pltpu.HBM((peers, 2 * frames, lat, width, features), BF16),
            pltpu.HBM((rows, 2 * features), BF16),
            pltpu.HBM((rows, 4 * features), BF16),
        ],
        scratch_shapes=[
            pltpu.VMEM((rows, 3 * features), BF16),
            pltpu.VMEM((rows, features), BF16),
        ],
        compiler_params=pltpu.CompilerParams(vmem_limit_bytes=56 << 20),
        cost_estimate=cost(18),
        name="temporal",
    )(mid, cot, gain, qkv, out)


def back_projection_kernel(dmid_ref, out_ref, dproj_ref):
    rows, features = dproj_ref.shape[1:]
    dmid = dmid_ref[...].astype(F32).reshape(rows, features).astype(BF16)
    dproj_ref[0] = dot(dmid, out_ref[...], 1, 1).astype(BF16)


def back_projection(dmid, out, frames):
    peers, _, each, width, features = dmid.shape
    rows = peers * each * width
    return pl.pallas_call(
        back_projection_kernel,
        grid=(frames,),
        in_specs=[grouped(peers, peers * each, width, features), full(out.shape)],
        out_specs=per_step((rows, features)),
        out_shape=pltpu.HBM((frames, rows, features), BF16),
        compiler_params=pltpu.CompilerParams(vmem_limit_bytes=12 << 20),
        cost_estimate=cost(30),
        name="back_projection",
    )(dmid, out)


def spatial_backward_kernel(
    dproj_ref, qkv_ref, q_ref, kv_ref, p_ref,
    dq_ref, dkv_ref, own_ref, west_ref, east_ref,
    acc_ref,
):
    _, lat, width, features = own_ref.shape
    rows = BH * width
    blocks = lat // BH
    step = 3 * rows
    mask = head_mask(rows)
    acc_ref[...] = jnp.zeros_like(acc_ref)
    offset = 0
    for b, (low, high) in enumerate(key_ranges(blocks, step)):
        span = high - low
        block = slice(b * rows, (b + 1) * rows)
        for g in range(features // LANES):
            lanes = slice(g * LANES, (g + 1) * LANES)
            late = slice(features + g * LANES, features + (g + 1) * LANES)
            queries = spread(q_ref[0, block, lanes], mask)
            d_out = spread(dproj_ref[0, block, lanes], mask)
            keys = kv_ref[0, low:high, lanes]
            values = kv_ref[0, low:high, late]
            weights = p_ref[0, g, offset : offset + span]
            wide = weights.astype(F32)
            d_weights = dot(values, d_out, 1, 1)
            delta = jnp.sum(wide * d_weights, axis=0, keepdims=True)
            d_scores = (wide * (d_weights - delta)).astype(BF16)
            d_query = gathered(dot(d_scores, keys, 0, 0), rows) * HDIM ** (-0.5)
            dq_ref[0, block, lanes] = d_query.astype(BF16)
            acc_ref[low:high, lanes] += dot(d_scores, queries)
            acc_ref[low:high, late] += dot(weights, d_out)
        offset += span
    dkv_ref[0] = acc_ref[...].astype(BF16)
    for b in range(blocks):
        part = slice(b * step, (b + 1) * step)
        d_y = dot(dkv_ref[0, part], qkv_ref[:, features:], 1, 1)
        block = slice(b * rows, (b + 1) * rows)
        d_own = d_y[rows : 2 * rows] + dot(dq_ref[0, block], qkv_ref[:, :features], 1, 1)
        for ref, value in ((west_ref, d_y[:rows]), (own_ref, d_own), (east_ref, d_y[2 * rows :])):
            ref[0, b * BH : (b + 1) * BH] = value.reshape(BH, width, features).astype(BF16)


def spatial_backward(dproj, qkv, q, kv, p, lat):
    frames, rows, features = dproj.shape
    width = rows // lat
    outs = (
        (rows, features),
        (3 * rows, 2 * features),
        (lat, width, features),
        (lat, width, features),
        (lat, width, features),
    )
    return pl.pallas_call(
        spatial_backward_kernel,
        grid=(frames,),
        in_specs=[
            per_step((rows, features)),
            full(qkv.shape),
            per_step(q.shape[1:]),
            per_step(kv.shape[1:]),
            per_step(p.shape[1:]),
        ],
        out_specs=[per_step(shape) for shape in outs],
        out_shape=[
            (pltpu.HBM if at >= 2 else jax.ShapeDtypeStruct)((frames,) + shape, BF16)
            for at, shape in enumerate(outs)
        ],
        scratch_shapes=[
            pltpu.VMEM((3 * rows, 2 * features), F32),
        ],
        compiler_params=pltpu.CompilerParams(vmem_limit_bytes=36 << 20),
        cost_estimate=cost(20),
        name="spatial_backward",
    )(*[from_hbm(a) for a in (dproj, qkv, q, kv, p)])


def final_kernel(tokens_ref, gain_ref, dmid_ref, own_ref, first_ref, second_ref, grad_ref):
    _, lat, width, features = tokens_ref.shape

    def flat(ref):
        return ref[0].astype(F32).reshape(lat * width, features)

    unit, inverse = normalized(flat(tokens_ref))
    d_y = flat(own_ref) + flat(first_ref) + flat(second_ref)
    d_mid = dmid_ref[...].astype(F32).reshape(lat * width, features)
    grad = d_mid + norm_back(unit, inverse, gain_ref[...], d_y)
    grad_ref[0] = grad.reshape(lat, width, features)


def final_norm(tokens, gain, dmid, own, first, second):
    frames, lat, width, features = tokens.shape
    block = per_step((lat, width, features))
    return pl.pallas_call(
        final_kernel,
        grid=(frames,),
        in_specs=[block, full((1, features)), grouped(dmid.shape[0], lat, width, features)]
        + [block] * 3,
        out_specs=block,
        out_shape=jax.ShapeDtypeStruct(tokens.shape, F32),
        compiler_params=pltpu.CompilerParams(vmem_limit_bytes=16 << 20),
        cost_estimate=cost(3),
        name="final_norm",
    )(tokens, gain, dmid, own, first, second)


def split_store(core_ref, term, keep_ref, send_ref):
    tiles, rows, columns = keep_ref.shape
    pairs = term.reshape(tiles, 2, rows, columns)
    first = core_ref[0] == 0
    for tile in range(tiles):
        even, odd = pairs[tile, 0], pairs[tile, 1]
        keep_ref[tile] = jnp.where(first, even, odd).astype(BF16)
        send_ref[tile] = jnp.where(first, odd, even).astype(BF16)


def term_time_kernel(core_ref, left_ref, right_ref, keep_ref, send_ref):
    split_store(core_ref, dot(left_ref[...], right_ref[...], 0, 0), keep_ref, send_ref)


def split_call(kernel, core, operands, specs, features, tiles, name, flops):
    shape = (tiles, features // (2 * tiles), 4 * features)
    block = pl.BlockSpec(shape[:2] + (features,), lambda i, core: (0, 0, i))
    return pl.pallas_call(
        kernel,
        grid_spec=pltpu.PrefetchScalarGridSpec(
            num_scalar_prefetch=1, grid=(4,), in_specs=specs, out_specs=[block, block]
        ),
        out_shape=[pltpu.HBM(shape, BF16)] * 2,
        compiler_params=pltpu.CompilerParams(vmem_limit_bytes=24 << 20),
        cost_estimate=pl.CostEstimate(flops=flops, bytes_accessed=1, transcendentals=0),
        name=name,
    )(core, *operands)


def term_time(core, left, right, tiles):
    rows, double = left.shape
    features = double // 2
    specs = [
        pl.BlockSpec((rows, features), lambda i, core: (0, i // 3)),
        pl.BlockSpec((rows, features), lambda i, core: (0, i)),
    ]
    return split_call(
        term_time_kernel, core, (from_hbm(left), from_hbm(right)), specs, features, tiles,
        "term_time", 1,
    )


def term_space_kernel(core_ref, y_ref, dq_ref, dkv_ref, o_ref, dmid_ref, keep_ref, send_ref):
    step = pl.program_id(0)
    frames, ext, features = y_ref.shape
    own = dq_ref.shape[1]

    @pl.when(step == 0)
    def _():
        part = BH * dmid_ref.shape[3]
        blocks = own // part
        pieces = [
            y_ref[f, (3 * b + 1) * part : (3 * b + 2) * part]
            for f in range(frames)
            for b in range(blocks)
        ]
        left = jnp.concatenate(pieces, axis=0)
        right = dq_ref[...].reshape(frames * own, features)
        split_store(core_ref, dot(left, right, 0, 0), keep_ref, send_ref)

    @pl.when((step == 1) | (step == 2))
    def _():
        left = y_ref[...].reshape(frames * ext, features)
        right = dkv_ref[...].reshape(frames * ext, features)
        split_store(core_ref, dot(left, right, 0, 0), keep_ref, send_ref)

    @pl.when(step == 3)
    def _():
        left = o_ref[...].reshape(frames * own, features)
        right = [dmid_ref[:, f].astype(F32).reshape(own, features) for f in range(frames)]
        right = jnp.concatenate(right, axis=0).astype(BF16)
        split_store(core_ref, dot(left, right, 0, 0), keep_ref, send_ref)


def term_space(core, y, dq, dkv, o, dmid, tiles):
    features = y.shape[-1]

    def whole(array):
        return pl.BlockSpec(
            array.shape, lambda i, core: (0,) * array.ndim, pipeline_mode=pl.Buffered(1)
        )

    specs = [
        whole(y),
        whole(dq),
        pl.BlockSpec(dkv.shape[:2] + (features,), lambda i, core: (0, 0, jnp.clip(i - 1, 0, 1))),
        whole(o),
        pl.BlockSpec(
            (dmid.shape[0], y.shape[0]) + dmid.shape[2:],
            lambda i, core: (0,) * dmid.ndim,
            pipeline_mode=pl.Buffered(1),
        ),
    ]
    return split_call(
        term_space_kernel, core, (y, dq, dkv, o, dmid), specs, features, tiles, "term_space", 1,
    )


def fold(total, row_ref, base, peers, put):
    rows, columns = total.shape
    across = columns // 128
    each = rows // peers
    for c in range(across):
        at = base + c * rows
        row_ref[at : at + rows] = total[:, c * 128 : (c + 1) * 128]
    for peer in range(peers):
        for r in range(0, each, 2):
            start = base + peer * each + r
            pair = [row_ref[pl.ds(start + k, across, stride=rows)] for k in range(2)]
            put(peer, slice(r * across, (r + 2) * across), jnp.concatenate(pair, axis=0).astype(BF16))


def pair_fold_kernel(peers, keep_ref, got_ref, sum_ref, row_ref):
    tiles, rows, columns = keep_ref.shape
    for tile in range(tiles):

        def put(peer, at, value):
            sum_ref[tile * peers + peer, at] = value

        total = keep_ref[tile].astype(F32) + got_ref[tile].astype(F32)
        fold(total, row_ref, tile * rows * columns // 128, peers, put)


def exchanged_pair(send):
    return lax.ppermute(send, "core", [(0, 1), (1, 0)])


def paired(keep, send, peers):
    got = exchanged_pair(send)
    tiles, rows, columns = keep.shape
    at_once = tiles // 4
    height = rows // peers * columns // 128
    block = pl.BlockSpec((at_once, rows, columns), lambda i: (i, 0, 0))
    return pl.pallas_call(
        functools.partial(pair_fold_kernel, peers),
        grid=(4,),
        in_specs=[block, block],
        out_specs=pl.BlockSpec((at_once * peers, height, 128), lambda i: (i, 0, 0)),
        out_shape=jax.ShapeDtypeStruct((tiles * peers, height, 128), BF16),
        scratch_shapes=[pltpu.VMEM((at_once * columns // 128 * rows, 128), F32)],
        compiler_params=pltpu.CompilerParams(vmem_limit_bytes=16 << 20),
        cost_estimate=pl.CostEstimate(flops=1, bytes_accessed=1, transcendentals=0),
        name="pair_fold",
    )(from_hbm(keep), got)


def sum_fold_kernel(arrived_ref, sum_ref, row_ref):
    def put(peer, at, value):
        sum_ref[peer, at] = value

    total = jnp.sum(arrived_ref[...].astype(F32), axis=0)
    fold(total, row_ref, 0, sum_ref.shape[0], put)


def sum_fold(arrived, peers):
    _, rows, columns = arrived.shape
    return pl.pallas_call(
        sum_fold_kernel,
        out_shape=jax.ShapeDtypeStruct((peers, rows // peers * columns // 128, 128), BF16),
        scratch_shapes=[pltpu.VMEM((columns // 128 * rows, 128), F32)],
        compiler_params=pltpu.CompilerParams(vmem_limit_bytes=16 << 20),
        cost_estimate=cost(3),
        name="sum_fold",
    )(arrived)


def ring_sum(chunks, axis):
    size = lax.axis_size(axis)
    me = lax.axis_index(axis).astype(jnp.uint32)

    def chunk(by):
        at = lax.bitwise_and(me + jnp.uint32(by), jnp.uint32(size - 1))
        return lax.dynamic_index_in_dim(chunks, at, 0, keepdims=False)

    total = chunk(0).astype(F32)
    for by in range(1, size):
        moved = lax.ppermute(chunk(by), axis, [(i, (i + by) % size) for i in range(size)])
        total = total + moved.astype(F32)
    return total


def summed_by_frame(chunks):
    z, xhi = lax.axis_size("z"), lax.axis_size("xhi")
    after_z = ring_sum(chunks.reshape((z, xhi) + chunks.shape[1:]), "z").astype(BF16)
    return ring_sum(after_z, "xhi")


def spread_out(mine):
    return lax.all_to_all(mine, ("xlo", "y", "z", "xhi"), 0, 0, tiled=False)


def shifted(shard, by):
    size = lax.axis_size(TILE)
    return lax.ppermute(shard, TILE, [(i, (i + by) % size) for i in range(size)])


def from_hbm(array):
    return pltpu.with_memory_space_constraint(array, pltpu.HBM)


def own_rows(weight):
    count = lax.axis_size(TILE + FRAME)
    per_device = weight.shape[0] // count
    at = lax.axis_index(TILE + FRAME) * per_device
    return lax.dynamic_slice_in_dim(weight, at, per_device, axis=0).astype(F32)


def finish_kernel(scale, arrived_ref, weight_ref, gain_ref, d_gain_ref, d_qkv_ref, d_out_ref):
    rows, wide = d_qkv_ref.shape
    total = jnp.sum(arrived_ref[...].astype(F32), axis=0) * scale
    across = total.shape[0] // rows
    own = wide // 128
    for r in range(rows):
        for c in range(across):
            part = total[r * across + c : r * across + c + 1]
            if c < own:
                d_qkv_ref[r : r + 1, c * 128 : (c + 1) * 128] = part
            else:
                d_out_ref[r : r + 1, (c - own) * 128 : (c - own + 1) * 128] = part
    along = jnp.sum(weight_ref[...] * d_qkv_ref[...], axis=1, keepdims=True)
    d_gain_ref[...] = along / gain_ref[...]


def finished(arrived, weight, gain, tokens):
    rows, wide = weight.shape
    features = arrived.shape[1] * 128 // rows - wide
    d_gain, d_qkv, d_out = pl.pallas_call(
        functools.partial(finish_kernel, 1.0 / math.sqrt(tokens)),
        out_shape=[
            jax.ShapeDtypeStruct((rows, 1), F32),
            jax.ShapeDtypeStruct((rows, wide), F32),
            jax.ShapeDtypeStruct((rows, features), F32),
        ],
        compiler_params=pltpu.CompilerParams(vmem_limit_bytes=12 << 20),
        cost_estimate=cost(2),
        name="finish",
    )(arrived, weight, gain.reshape(rows, 1))
    return d_gain.reshape(rows), d_qkv, d_out


def shards(tokens, gain_space, qkv_space, out_space, gain_time, qkv_time, out_time, cotangent):
    frames, lat, width, features = tokens.shape
    total = frames * lat * width * lax.axis_size(TILE) * lax.axis_size(FRAME)
    gain_s = gain_space.reshape(1, features)
    gain_t = gain_time.reshape(1, features)
    core = lax.axis_index("core").astype(jnp.int32).reshape(1)
    tiles = lax.axis_size(("xlo", "y"))

    peers = lax.axis_size(FRAME)

    def exchanged(chunks):
        return lax.all_to_all(chunks, FRAME, 0, 0, tiled=False)

    west = shifted(tokens, 1)
    east = shifted(tokens, -1)
    cot_chunks = cotangent.reshape(frames, peers, lat // peers, width, features)
    cot_rows = exchanged(cot_chunks.transpose(1, 0, 2, 3, 4))
    y_s, q_s, kv_s, p_s, o_s, mid = spatial_forward(
        tokens, west, east, gain_s, qkv_space, out_space, peers
    )
    both_rows, left_t, right_t = temporal(exchanged(mid), cot_rows, gain_t, qkv_time, out_time)
    both = exchanged(both_rows)
    keep_t, send_t = term_time(core, left_t, right_t, tiles)
    mine_t = (keep_t.astype(F32) + exchanged_pair(send_t).astype(F32)).astype(BF16)
    dproj = back_projection(both, out_space, frames)
    dproj, mine_t = lax.optimization_barrier((dproj, mine_t))
    arrived_t = lax.all_to_all(mine_t, ("xlo", "y"), 0, 0, tiled=False)
    dq, dkv, own, for_west, for_east = spatial_backward(dproj, qkv_space, q_s, kv_s, p_s, lat)
    from_east = shifted(for_west, -1)
    from_west = shifted(for_east, 1)
    keep_s, send_s = term_space(core, y_s, dq, dkv, o_s, both, tiles)
    send_s, arrived_t = lax.optimization_barrier((send_s, arrived_t))
    arrived_s = spread_out(paired(keep_s, send_s, peers))
    summed_t = summed_by_frame(sum_fold(arrived_t, peers))[None]
    layer_out = both[:, frames:].transpose(1, 0, 2, 3, 4).reshape(tokens.shape)
    grad_tokens = final_norm(tokens, gain_s, both, own, from_east, from_west)
    return (
        (layer_out, grad_tokens)
        + finished(arrived_s, own_rows(qkv_space), own_rows(gain_space), total)
        + finished(summed_t, own_rows(qkv_time), own_rows(gain_time), total)
    )


def solution(mesh):
    fine = Mesh(mesh.devices.reshape(2, 4, 2, 4, 2), TILE + FRAME)
    token_spec = P(FRAME, None, TILE, None)
    row_spec = P(TILE + FRAME)
    return jax.shard_map(
        shards,
        mesh=fine,
        in_specs=(token_spec, P(), P(), P(), P(), P(), P(), token_spec),
        out_specs=(token_spec, token_spec) + (row_spec,) * 6,
        check_vma=False,
    )
```

```python
import functools
import math

import jax
import jax.numpy as jnp
from jax import lax
from jax.experimental import pallas as pl
from jax.experimental.pallas import tpu as pltpu
from jax.sharding import Mesh
from jax.sharding import PartitionSpec as P

HDIM = 64
BH = 8
LANES = 4 * HDIM
EPS = 1e-05
F32 = jnp.float32
BF16 = jnp.bfloat16
TILE = ("xlo", "y", "core")
FRAME = ("z", "xhi")


def dot(left, right, left_dim=1, right_dim=0):
    return lax.dot_general(
        left, right, (((left_dim,), (right_dim,)), ((), ())), preferred_element_type=F32
    )


def normalized(rows):
    centred = rows - jnp.mean(rows, axis=-1, keepdims=True)
    variance = jnp.mean(centred * centred, axis=-1, keepdims=True)
    inverse = lax.rsqrt(variance + EPS)
    return centred * inverse, inverse


def norm_back(unit, inverse, gain, d_out):
    d_unit = d_out * gain
    along = jnp.mean(d_unit * unit, axis=-1, keepdims=True)
    return inverse * (d_unit - jnp.mean(d_unit, axis=-1, keepdims=True) - unit * along)


def head_mask(rows):
    row_head = lax.broadcasted_iota(jnp.int32, (4 * rows, LANES), 0) // rows
    lane_head = lax.broadcasted_iota(jnp.int32, (4 * rows, LANES), 1) // HDIM
    return row_head == lane_head


def spread(group, mask):
    stacked = jnp.concatenate([group] * 4, axis=0)
    return jnp.where(mask, stacked, jnp.zeros_like(stacked))


def gathered(wide, rows):
    lane_head = lax.broadcasted_iota(jnp.int32, (rows, LANES), 1) // HDIM
    parts = [wide[h * rows : (h + 1) * rows] for h in range(4)]
    low = jnp.where(lane_head == 0, parts[0], parts[1])
    high = jnp.where(lane_head == 2, parts[2], parts[3])
    return jnp.where(lane_head < 2, low, high)


def softmax_rows(scores):
    top = jnp.max(scores, axis=0, keepdims=True)
    exponent = jnp.exp(scores - top)
    return exponent * (1.0 / jnp.sum(exponent, axis=0, keepdims=True))


def key_ranges(blocks, step):
    return [(max(b - 1, 0) * step, min(b + 2, blocks) * step) for b in range(blocks)]


def spatial_forward_kernel(
    own_ref, west_ref, east_ref, gain_ref, qkv_ref, out_ref,
    y_ref, q_ref, kv_ref, p_ref, o_ref, mid_ref,
):
    _, lat, width, features = own_ref.shape
    rows = BH * width
    blocks = lat // BH
    step = 3 * rows
    gain = gain_ref[...]
    for tile, ref in enumerate((west_ref, own_ref, east_ref)):
        wide = ref[0].astype(F32).reshape(lat * width, features)
        unit, _ = normalized(wide)
        y = (unit * gain).astype(BF16)
        for b in range(blocks):
            at = b * step + tile * rows
            y_ref[0, at : at + rows] = y[b * rows : (b + 1) * rows]
        if tile == 1:
            q_ref[0] = (dot(y, qkv_ref[:, :features]).astype(BF16) * HDIM ** (-0.5)).astype(BF16)
    for b in range(blocks):
        part = slice(b * step, (b + 1) * step)
        kv_ref[0, part] = dot(y_ref[0, part], qkv_ref[:, features:]).astype(BF16)
    mask = head_mask(rows)
    offset = 0
    for b, (low, high) in enumerate(key_ranges(blocks, step)):
        span = high - low
        for g in range(features // LANES):
            lanes = slice(g * LANES, (g + 1) * LANES)
            queries = spread(q_ref[0, b * rows : (b + 1) * rows, lanes], mask)
            keys = kv_ref[0, low:high, lanes]
            values = kv_ref[0, low:high, features + g * LANES : features + (g + 1) * LANES]
            weights = softmax_rows(dot(keys, queries, 1, 1)).astype(BF16)
            p_ref[0, g, offset : offset + span] = weights
            mixed = dot(weights, values, 0, 0)
            o_ref[0, b * rows : (b + 1) * rows, lanes] = gathered(mixed, rows).astype(BF16)
        offset += span
    wide = own_ref[0].astype(F32).reshape(lat * width, features)
    mid = wide + dot(o_ref[0], out_ref[...])
    mid_ref[:, 0] = mid.reshape(-1, mid_ref.shape[2], width, features).astype(BF16)


def full(shape):
    return pl.BlockSpec(shape, lambda *_: (0,) * len(shape), pipeline_mode=pl.Buffered(1))


def per_step(shape):
    return pl.BlockSpec((1,) + shape, lambda i: (i,) + (0,) * len(shape))


def cost(microseconds):
    return pl.CostEstimate(
        flops=microseconds * 10**9, bytes_accessed=4 << 20, transcendentals=2 * 10**6
    )


def grouped(peers, lat, width, features):
    return pl.BlockSpec((peers, 1, lat // peers, width, features), lambda i: (0, i, 0, 0, 0))


def spatial_forward(own, west, east, gain, qkv, out, peers):
    frames, lat, width, features = own.shape
    rows = lat * width
    blocks = lat // BH
    spans = sum(h - l for l, h in key_ranges(blocks, 3 * BH * width))
    groups = features // LANES
    outs = (
        ((3 * rows, features), BF16),
        ((rows, features), BF16),
        ((3 * rows, 2 * features), BF16),
        ((groups, spans, LANES), BF16),
        ((rows, features), BF16),
    )
    mid_shape = (peers, frames, lat // peers, width, features)
    return pl.pallas_call(
        spatial_forward_kernel,
        grid=(frames,),
        in_specs=[per_step((lat, width, features))] * 3
        + [full((1, features)), full(qkv.shape), full(out.shape)],
        out_specs=[per_step(shape) for shape, _ in outs] + [grouped(peers, lat, width, features)],
        out_shape=[pltpu.HBM((frames,) + shape, kind) for shape, kind in outs]
        + [pltpu.HBM(mid_shape, BF16)],
        compiler_params=pltpu.CompilerParams(vmem_limit_bytes=36 << 20),
        cost_estimate=cost(14),
        name="spatial_forward",
    )(*[from_hbm(a) for a in (own, west, east)], gain, from_hbm(qkv), from_hbm(out))


def temporal_kernel(
    mid_ref, cot_ref, gain_ref, qkv_ref, out_ref,
    both_ref, left_ref, right_ref,
    packed_ref, dproj_ref,
):
    peers, frames, lat, width, features = mid_ref.shape
    rows = peers * frames * width
    gain = gain_ref[...]
    scale = HDIM ** (-0.5)

    def by_row(ref, row):
        return ref[:, :, row].astype(F32).reshape(rows, features)

    for row in range(lat):
        part = slice(row * rows, (row + 1) * rows)
        unit, _ = normalized(by_row(mid_ref, row))
        left_ref[part, :features] = (unit * gain).astype(BF16)
        right_ref[part, 3 * features :] = by_row(cot_ref, row).astype(BF16)
    packed_ref[...] = dot(left_ref[:, :features], qkv_ref[...]).astype(BF16)
    dproj_ref[...] = dot(right_ref[:, 3 * features :], out_ref[...], 1, 1).astype(BF16)
    mask = head_mask(rows)
    key_col = lax.broadcasted_iota(jnp.int32, (rows, 4 * rows), 0) % width
    query_col = lax.broadcasted_iota(jnp.int32, (rows, 4 * rows), 1) % width
    same = key_col == query_col
    for row in range(lat):
        part = slice(row * rows, (row + 1) * rows)
        for g in range(features // LANES):
            lanes = [
                slice(s * features + g * LANES, s * features + (g + 1) * LANES) for s in range(3)
            ]
            queries = spread((packed_ref[part, lanes[0]] * scale).astype(BF16), mask)
            keys = packed_ref[part, lanes[1]]
            values = packed_ref[part, lanes[2]]
            scores = jnp.where(same, dot(keys, queries, 1, 1), -1e30)
            wide = softmax_rows(scores)
            weights = wide.astype(BF16)
            mixed = dot(weights, values, 0, 0)
            left_ref[part, lanes[1]] = gathered(mixed, rows).astype(BF16)
            d_out = spread(dproj_ref[part, lanes[0]], mask)
            d_weights = dot(values, d_out, 1, 1)
            delta = jnp.sum(wide * d_weights, axis=0, keepdims=True)
            d_scores = (wide * (d_weights - delta)).astype(BF16)
            d_query = gathered(dot(d_scores, keys, 0, 0), rows) * scale
            right_ref[part, lanes[0]] = d_query.astype(BF16)
            right_ref[part, lanes[1]] = dot(d_scores, queries).astype(BF16)
            right_ref[part, lanes[2]] = dot(weights, d_out).astype(BF16)
    layer = dot(left_ref[:, features:], out_ref[...])
    d_y = dot(right_ref[:, : 3 * features], qkv_ref[...], 1, 1)
    shape = (peers, frames, width, features)
    for row in range(lat):
        part = slice(row * rows, (row + 1) * rows)
        mid = by_row(mid_ref, row)
        unit, inverse = normalized(mid)
        d_mid = by_row(cot_ref, row) + norm_back(unit, inverse, gain, d_y[part])
        both_ref[:, :frames, row] = d_mid.reshape(shape).astype(BF16)
        both_ref[:, frames:, row] = (mid + layer[part]).reshape(shape).astype(BF16)


def temporal(mid, cot, gain, qkv, out):
    peers, frames, lat, width, features = mid.shape
    rows = peers * frames * lat * width
    return pl.pallas_call(
        temporal_kernel,
        out_shape=[
            pltpu.HBM((peers, 2 * frames, lat, width, features), BF16),
            pltpu.HBM((rows, 2 * features), BF16),
            pltpu.HBM((rows, 4 * features), BF16),
        ],
        scratch_shapes=[
            pltpu.VMEM((rows, 3 * features), BF16),
            pltpu.VMEM((rows, features), BF16),
        ],
        compiler_params=pltpu.CompilerParams(vmem_limit_bytes=56 << 20),
        cost_estimate=cost(18),
        name="temporal",
    )(mid, cot, gain, qkv, out)


def back_projection_kernel(dmid_ref, out_ref, dproj_ref):
    rows, features = dproj_ref.shape[1:]
    dmid = dmid_ref[...].astype(F32).reshape(rows, features).astype(BF16)
    dproj_ref[0] = dot(dmid, out_ref[...], 1, 1).astype(BF16)


def back_projection(dmid, out, frames):
    peers, _, each, width, features = dmid.shape
    rows = peers * each * width
    return pl.pallas_call(
        back_projection_kernel,
        grid=(frames,),
        in_specs=[grouped(peers, peers * each, width, features), full(out.shape)],
        out_specs=per_step((rows, features)),
        out_shape=pltpu.HBM((frames, rows, features), BF16),
        compiler_params=pltpu.CompilerParams(vmem_limit_bytes=12 << 20),
        cost_estimate=cost(30),
        name="back_projection",
    )(dmid, out)


def spatial_backward_kernel(
    dproj_ref, qkv_ref, q_ref, kv_ref, p_ref,
    dq_ref, dkv_ref, own_ref, west_ref, east_ref,
    acc_ref,
):
    _, lat, width, features = own_ref.shape
    rows = BH * width
    blocks = lat // BH
    step = 3 * rows
    mask = head_mask(rows)
    acc_ref[...] = jnp.zeros_like(acc_ref)
    offset = 0
    for b, (low, high) in enumerate(key_ranges(blocks, step)):
        span = high - low
        block = slice(b * rows, (b + 1) * rows)
        for g in range(features // LANES):
            lanes = slice(g * LANES, (g + 1) * LANES)
            late = slice(features + g * LANES, features + (g + 1) * LANES)
            queries = spread(q_ref[0, block, lanes], mask)
            d_out = spread(dproj_ref[0, block, lanes], mask)
            keys = kv_ref[0, low:high, lanes]
            values = kv_ref[0, low:high, late]
            weights = p_ref[0, g, offset : offset + span]
            wide = weights.astype(F32)
            d_weights = dot(values, d_out, 1, 1)
            delta = jnp.sum(wide * d_weights, axis=0, keepdims=True)
            d_scores = (wide * (d_weights - delta)).astype(BF16)
            d_query = gathered(dot(d_scores, keys, 0, 0), rows) * HDIM ** (-0.5)
            dq_ref[0, block, lanes] = d_query.astype(BF16)
            acc_ref[low:high, lanes] += dot(d_scores, queries)
            acc_ref[low:high, late] += dot(weights, d_out)
        offset += span
    dkv_ref[0] = acc_ref[...].astype(BF16)
    for b in range(blocks):
        part = slice(b * step, (b + 1) * step)
        d_y = dot(dkv_ref[0, part], qkv_ref[:, features:], 1, 1)
        block = slice(b * rows, (b + 1) * rows)
        d_own = d_y[rows : 2 * rows] + dot(dq_ref[0, block], qkv_ref[:, :features], 1, 1)
        for ref, value in ((west_ref, d_y[:rows]), (own_ref, d_own), (east_ref, d_y[2 * rows :])):
            ref[0, b * BH : (b + 1) * BH] = value.reshape(BH, width, features).astype(BF16)


def spatial_backward(dproj, qkv, q, kv, p, lat):
    frames, rows, features = dproj.shape
    width = rows // lat
    outs = (
        (rows, features),
        (3 * rows, 2 * features),
        (lat, width, features),
        (lat, width, features),
        (lat, width, features),
    )
    return pl.pallas_call(
        spatial_backward_kernel,
        grid=(frames,),
        in_specs=[
            per_step((rows, features)),
            full(qkv.shape),
            per_step(q.shape[1:]),
            per_step(kv.shape[1:]),
            per_step(p.shape[1:]),
        ],
        out_specs=[per_step(shape) for shape in outs],
        out_shape=[
            (pltpu.HBM if at >= 2 else jax.ShapeDtypeStruct)((frames,) + shape, BF16)
            for at, shape in enumerate(outs)
        ],
        scratch_shapes=[
            pltpu.VMEM((3 * rows, 2 * features), F32),
        ],
        compiler_params=pltpu.CompilerParams(vmem_limit_bytes=36 << 20),
        cost_estimate=cost(20),
        name="spatial_backward",
    )(*[from_hbm(a) for a in (dproj, qkv, q, kv, p)])


def final_kernel(tokens_ref, gain_ref, dmid_ref, own_ref, first_ref, second_ref, grad_ref):
    _, lat, width, features = tokens_ref.shape

    def flat(ref):
        return ref[0].astype(F32).reshape(lat * width, features)

    unit, inverse = normalized(flat(tokens_ref))
    d_y = flat(own_ref) + flat(first_ref) + flat(second_ref)
    d_mid = dmid_ref[...].astype(F32).reshape(lat * width, features)
    grad = d_mid + norm_back(unit, inverse, gain_ref[...], d_y)
    grad_ref[0] = grad.reshape(lat, width, features)


def final_norm(tokens, gain, dmid, own, first, second):
    frames, lat, width, features = tokens.shape
    block = per_step((lat, width, features))
    return pl.pallas_call(
        final_kernel,
        grid=(frames,),
        in_specs=[block, full((1, features)), grouped(dmid.shape[0], lat, width, features)]
        + [block] * 3,
        out_specs=block,
        out_shape=jax.ShapeDtypeStruct(tokens.shape, F32),
        compiler_params=pltpu.CompilerParams(vmem_limit_bytes=16 << 20),
        cost_estimate=cost(3),
        name="final_norm",
    )(tokens, gain, dmid, own, first, second)


def split_store(core_ref, term, keep_ref, send_ref):
    tiles, rows, columns = keep_ref.shape
    pairs = term.reshape(tiles, 2, rows, columns)
    first = core_ref[0] == 0
    for tile in range(tiles):
        even, odd = pairs[tile, 0], pairs[tile, 1]
        keep_ref[tile] = jnp.where(first, even, odd).astype(BF16)
        send_ref[tile] = jnp.where(first, odd, even).astype(BF16)


def term_time_kernel(core_ref, left_ref, right_ref, keep_ref, send_ref):
    split_store(core_ref, dot(left_ref[...], right_ref[...], 0, 0), keep_ref, send_ref)


def split_call(kernel, core, operands, specs, features, tiles, name, flops):
    shape = (tiles, features // (2 * tiles), 4 * features)
    block = pl.BlockSpec(shape[:2] + (features,), lambda i, core: (0, 0, i))
    return pl.pallas_call(
        kernel,
        grid_spec=pltpu.PrefetchScalarGridSpec(
            num_scalar_prefetch=1, grid=(4,), in_specs=specs, out_specs=[block, block]
        ),
        out_shape=[pltpu.HBM(shape, BF16)] * 2,
        compiler_params=pltpu.CompilerParams(vmem_limit_bytes=24 << 20),
        cost_estimate=pl.CostEstimate(flops=flops, bytes_accessed=1, transcendentals=0),
        name=name,
    )(core, *operands)


def term_time(core, left, right, tiles):
    rows, double = left.shape
    features = double // 2
    specs = [
        pl.BlockSpec((rows, features), lambda i, core: (0, i // 3)),
        pl.BlockSpec((rows, features), lambda i, core: (0, i)),
    ]
    return split_call(
        term_time_kernel, core, (from_hbm(left), from_hbm(right)), specs, features, tiles,
        "term_time", 1,
    )


def term_space_kernel(core_ref, y_ref, dq_ref, dkv_ref, o_ref, dmid_ref, keep_ref, send_ref):
    step = pl.program_id(0)
    frames, ext, features = y_ref.shape
    own = dq_ref.shape[1]

    @pl.when(step == 0)
    def _():
        part = BH * dmid_ref.shape[3]
        blocks = own // part
        pieces = [
            y_ref[f, (3 * b + 1) * part : (3 * b + 2) * part]
            for f in range(frames)
            for b in range(blocks)
        ]
        left = jnp.concatenate(pieces, axis=0)
        right = dq_ref[...].reshape(frames * own, features)
        split_store(core_ref, dot(left, right, 0, 0), keep_ref, send_ref)

    @pl.when((step == 1) | (step == 2))
    def _():
        left = y_ref[...].reshape(frames * ext, features)
        right = dkv_ref[...].reshape(frames * ext, features)
        split_store(core_ref, dot(left, right, 0, 0), keep_ref, send_ref)

    @pl.when(step == 3)
    def _():
        left = o_ref[...].reshape(frames * own, features)
        right = [dmid_ref[:, f].astype(F32).reshape(own, features) for f in range(frames)]
        right = jnp.concatenate(right, axis=0).astype(BF16)
        split_store(core_ref, dot(left, right, 0, 0), keep_ref, send_ref)


def term_space(core, y, dq, dkv, o, dmid, tiles):
    features = y.shape[-1]

    def whole(array):
        return pl.BlockSpec(
            array.shape, lambda i, core: (0,) * array.ndim, pipeline_mode=pl.Buffered(1)
        )

    specs = [
        whole(y),
        whole(dq),
        pl.BlockSpec(dkv.shape[:2] + (features,), lambda i, core: (0, 0, jnp.clip(i - 1, 0, 1))),
        whole(o),
        pl.BlockSpec(
            (dmid.shape[0], y.shape[0]) + dmid.shape[2:],
            lambda i, core: (0,) * dmid.ndim,
            pipeline_mode=pl.Buffered(1),
        ),
    ]
    return split_call(
        term_space_kernel, core, (y, dq, dkv, o, dmid), specs, features, tiles, "term_space", 1,
    )


def fold(total, row_ref, base, peers, put):
    rows, columns = total.shape
    across = columns // 128
    each = rows // peers
    for c in range(across):
        at = base + c * rows
        row_ref[at : at + rows] = total[:, c * 128 : (c + 1) * 128]
    for peer in range(peers):
        for r in range(0, each, 2):
            start = base + peer * each + r
            pair = [row_ref[pl.ds(start + k, across, stride=rows)] for k in range(2)]
            put(peer, slice(r * across, (r + 2) * across), jnp.concatenate(pair, axis=0).astype(BF16))


def pair_fold_kernel(peers, keep_ref, got_ref, sum_ref, row_ref):
    tiles, rows, columns = keep_ref.shape
    for tile in range(tiles):

        def put(peer, at, value):
            sum_ref[tile * peers + peer, at] = value

        total = keep_ref[tile].astype(F32) + got_ref[tile].astype(F32)
        fold(total, row_ref, tile * rows * columns // 128, peers, put)


def exchanged_pair(send):
    return lax.ppermute(send, "core", [(0, 1), (1, 0)])


def paired(keep, send, peers):
    got = exchanged_pair(send)
    tiles, rows, columns = keep.shape
    at_once = tiles // 4
    height = rows // peers * columns // 128
    block = pl.BlockSpec((at_once, rows, columns), lambda i: (i, 0, 0))
    return pl.pallas_call(
        functools.partial(pair_fold_kernel, peers),
        grid=(4,),
        in_specs=[block, block],
        out_specs=pl.BlockSpec((at_once * peers, height, 128), lambda i: (i, 0, 0)),
        out_shape=jax.ShapeDtypeStruct((tiles * peers, height, 128), BF16),
        scratch_shapes=[pltpu.VMEM((at_once * columns // 128 * rows, 128), F32)],
        compiler_params=pltpu.CompilerParams(vmem_limit_bytes=16 << 20),
        cost_estimate=pl.CostEstimate(flops=1, bytes_accessed=1, transcendentals=0),
        name="pair_fold",
    )(from_hbm(keep), got)


def sum_fold_kernel(arrived_ref, sum_ref, row_ref):
    def put(peer, at, value):
        sum_ref[peer, at] = value

    total = jnp.sum(arrived_ref[...].astype(F32), axis=0)
    fold(total, row_ref, 0, sum_ref.shape[0], put)


def sum_fold(arrived, peers):
    _, rows, columns = arrived.shape
    return pl.pallas_call(
        sum_fold_kernel,
        out_shape=pltpu.HBM((peers, rows // peers * columns // 128, 128), BF16),
        scratch_shapes=[pltpu.VMEM((columns // 128 * rows, 128), F32)],
        compiler_params=pltpu.CompilerParams(vmem_limit_bytes=16 << 20),
        cost_estimate=pl.CostEstimate(flops=1, bytes_accessed=1, transcendentals=0),
        name="sum_fold",
    )(arrived)


def ring_sum(chunks, axis):
    size = lax.axis_size(axis)
    me = lax.axis_index(axis).astype(jnp.uint32)

    def chunk(by):
        at = lax.bitwise_and(me + jnp.uint32(by), jnp.uint32(size - 1))
        return lax.dynamic_index_in_dim(chunks, at, 0, keepdims=False)

    total = chunk(0).astype(F32)
    for by in range(1, size):
        moved = lax.ppermute(chunk(by), axis, [(i, (i + by) % size) for i in range(size)])
        total = total + moved.astype(F32)
    return total


def summed_by_frame(chunks):
    z, xhi = lax.axis_size("z"), lax.axis_size("xhi")
    after_z = ring_sum(chunks.reshape((z, xhi) + chunks.shape[1:]), "z").astype(BF16)
    return ring_sum(after_z, "xhi")


def spread_out(mine):
    return lax.all_to_all(mine, ("xlo", "y", "z", "xhi"), 0, 0, tiled=False)


def shifted(shard, by):
    size = lax.axis_size(TILE)
    return lax.ppermute(shard, TILE, [(i, (i + by) % size) for i in range(size)])


def from_hbm(array):
    return pltpu.with_memory_space_constraint(array, pltpu.HBM)


def own_rows(weight):
    count = lax.axis_size(TILE + FRAME)
    per_device = weight.shape[0] // count
    at = lax.axis_index(TILE + FRAME) * per_device
    return lax.dynamic_slice_in_dim(weight, at, per_device, axis=0).astype(F32)


def finish_kernel(scale, arrived_ref, weight_ref, gain_ref, d_gain_ref, d_qkv_ref, d_out_ref):
    rows, wide = d_qkv_ref.shape
    total = jnp.sum(arrived_ref[...].astype(F32), axis=0) * scale
    across = total.shape[0] // rows
    own = wide // 128
    for r in range(rows):
        for c in range(across):
            part = total[r * across + c : r * across + c + 1]
            if c < own:
                d_qkv_ref[r : r + 1, c * 128 : (c + 1) * 128] = part
            else:
                d_out_ref[r : r + 1, (c - own) * 128 : (c - own + 1) * 128] = part
    along = jnp.sum(weight_ref[...] * d_qkv_ref[...], axis=1, keepdims=True)
    d_gain_ref[...] = along / gain_ref[...]


def finished(arrived, weight, gain, tokens):
    rows, wide = weight.shape
    features = arrived.shape[1] * 128 // rows - wide
    d_gain, d_qkv, d_out = pl.pallas_call(
        functools.partial(finish_kernel, 1.0 / math.sqrt(tokens)),
        out_shape=[
            jax.ShapeDtypeStruct((rows, 1), F32),
            jax.ShapeDtypeStruct((rows, wide), F32),
            jax.ShapeDtypeStruct((rows, features), F32),
        ],
        compiler_params=pltpu.CompilerParams(vmem_limit_bytes=12 << 20),
        cost_estimate=cost(2),
        name="finish",
    )(arrived, weight, gain.reshape(rows, 1))
    return d_gain.reshape(rows), d_qkv, d_out


def shards(tokens, gain_space, qkv_space, out_space, gain_time, qkv_time, out_time, cotangent):
    frames, lat, width, features = tokens.shape
    total = frames * lat * width * lax.axis_size(TILE) * lax.axis_size(FRAME)
    gain_s = gain_space.reshape(1, features)
    gain_t = gain_time.reshape(1, features)
    core = lax.axis_index("core").astype(jnp.int32).reshape(1)
    tiles = lax.axis_size(("xlo", "y"))

    peers = lax.axis_size(FRAME)

    def exchanged(chunks):
        return lax.all_to_all(chunks, FRAME, 0, 0, tiled=False)

    west = shifted(tokens, 1)
    east = shifted(tokens, -1)
    cot_chunks = cotangent.reshape(frames, peers, lat // peers, width, features)
    cot_rows = exchanged(cot_chunks.transpose(1, 0, 2, 3, 4))
    y_s, q_s, kv_s, p_s, o_s, mid = spatial_forward(
        tokens, west, east, gain_s, qkv_space, out_space, peers
    )
    slices = [own_rows(a) for a in (qkv_space, gain_space, qkv_time, gain_time)]
    mid, cot_rows = lax.optimization_barrier((mid, cot_rows))
    mid_rows, slices = lax.optimization_barrier((exchanged(mid), slices))
    both_rows, left_t, right_t = temporal(mid_rows, cot_rows, gain_t, qkv_time, out_time)
    both = exchanged(both_rows)
    keep_t, send_t = term_time(core, left_t, right_t, tiles)
    mine_t = (keep_t.astype(F32) + exchanged_pair(send_t).astype(F32)).astype(BF16)
    dproj = back_projection(both, out_space, frames)
    dproj, mine_t = lax.optimization_barrier((dproj, mine_t))
    arrived_t = lax.all_to_all(mine_t, ("xlo", "y"), 0, 0, tiled=False)
    dq, dkv, own, for_west, for_east = spatial_backward(dproj, qkv_space, q_s, kv_s, p_s, lat)
    from_east = shifted(for_west, -1)
    from_west = shifted(for_east, 1)
    keep_s, send_s = term_space(core, y_s, dq, dkv, o_s, both, tiles)
    folded_t = sum_fold(arrived_t, peers)
    send_s, folded_t = lax.optimization_barrier((send_s, folded_t))
    arrived_s = spread_out(paired(keep_s, send_s, peers))
    summed_t = summed_by_frame(folded_t)[None]
    layer_out = both[:, frames:].transpose(1, 0, 2, 3, 4).reshape(tokens.shape)
    grad_tokens = final_norm(tokens, gain_s, both, own, from_east, from_west)
    return (
        (layer_out, grad_tokens)
        + finished(arrived_s, slices[0], slices[1], total)
        + finished(summed_t, slices[2], slices[3], total)
    )


def solution(mesh):
    fine = Mesh(mesh.devices.reshape(2, 4, 2, 4, 2), TILE + FRAME)
    token_spec = P(FRAME, None, TILE, None)
    row_spec = P(TILE + FRAME)
    return jax.shard_map(
        shards,
        mesh=fine,
        in_specs=(token_spec, P(), P(), P(), P(), P(), P(), token_spec),
        out_specs=(token_spec, token_spec) + (row_spec,) * 6,
        check_vma=False,
    )
```

```python
import functools
import math

import jax
import jax.numpy as jnp
from jax import lax
from jax.experimental import pallas as pl
from jax.experimental.pallas import tpu as pltpu
from jax.sharding import Mesh
from jax.sharding import PartitionSpec as P

HDIM = 64
BH = 8
LANES = 4 * HDIM
EPS = 1e-05
F32 = jnp.float32
BF16 = jnp.bfloat16
TILE = ("xlo", "y", "core")
FRAME = ("z", "xhi")


def dot(left, right, left_dim=1, right_dim=0):
    return lax.dot_general(
        left, right, (((left_dim,), (right_dim,)), ((), ())), preferred_element_type=F32
    )


def normalized(rows):
    centred = rows - jnp.mean(rows, axis=-1, keepdims=True)
    variance = jnp.mean(centred * centred, axis=-1, keepdims=True)
    inverse = lax.rsqrt(variance + EPS)
    return centred * inverse, inverse


def norm_back(unit, inverse, gain, d_out):
    d_unit = d_out * gain
    along = jnp.mean(d_unit * unit, axis=-1, keepdims=True)
    return inverse * (d_unit - jnp.mean(d_unit, axis=-1, keepdims=True) - unit * along)


def head_mask(rows):
    row_head = lax.broadcasted_iota(jnp.int32, (4 * rows, LANES), 0) // rows
    lane_head = lax.broadcasted_iota(jnp.int32, (4 * rows, LANES), 1) // HDIM
    return row_head == lane_head


def spread(group, mask):
    stacked = jnp.concatenate([group] * 4, axis=0)
    return jnp.where(mask, stacked, jnp.zeros_like(stacked))


def gathered(wide, rows):
    lane_head = lax.broadcasted_iota(jnp.int32, (rows, LANES), 1) // HDIM
    parts = [wide[h * rows : (h + 1) * rows] for h in range(4)]
    low = jnp.where(lane_head == 0, parts[0], parts[1])
    high = jnp.where(lane_head == 2, parts[2], parts[3])
    return jnp.where(lane_head < 2, low, high)


def softmax_rows(scores):
    top = jnp.max(scores, axis=0, keepdims=True)
    exponent = jnp.exp(scores - top)
    return exponent * (1.0 / jnp.sum(exponent, axis=0, keepdims=True))


def key_ranges(blocks, step):
    return [(max(b - 1, 0) * step, min(b + 2, blocks) * step) for b in range(blocks)]


def spatial_forward_kernel(
    own_ref, west_ref, east_ref, gain_ref, qkv_ref, out_ref,
    y_ref, q_ref, kv_ref, p_ref, o_ref, mid_ref,
):
    _, lat, width, features = own_ref.shape
    rows = BH * width
    blocks = lat // BH
    step = 3 * rows
    gain = gain_ref[...]
    for tile, ref in enumerate((west_ref, own_ref, east_ref)):
        wide = ref[0].astype(F32).reshape(lat * width, features)
        unit, _ = normalized(wide)
        y = (unit * gain).astype(BF16)
        for b in range(blocks):
            at = b * step + tile * rows
            y_ref[0, at : at + rows] = y[b * rows : (b + 1) * rows]
        if tile == 1:
            q_ref[0] = (dot(y, qkv_ref[:, :features]).astype(BF16) * HDIM ** (-0.5)).astype(BF16)
    for b in range(blocks):
        part = slice(b * step, (b + 1) * step)
        kv_ref[0, part] = dot(y_ref[0, part], qkv_ref[:, features:]).astype(BF16)
    mask = head_mask(rows)
    offset = 0
    for b, (low, high) in enumerate(key_ranges(blocks, step)):
        span = high - low
        for g in range(features // LANES):
            lanes = slice(g * LANES, (g + 1) * LANES)
            queries = spread(q_ref[0, b * rows : (b + 1) * rows, lanes], mask)
            keys = kv_ref[0, low:high, lanes]
            values = kv_ref[0, low:high, features + g * LANES : features + (g + 1) * LANES]
            weights = softmax_rows(dot(keys, queries, 1, 1)).astype(BF16)
            p_ref[0, g, offset : offset + span] = weights
            mixed = dot(weights, values, 0, 0)
            o_ref[0, b * rows : (b + 1) * rows, lanes] = gathered(mixed, rows).astype(BF16)
        offset += span
    wide = own_ref[0].astype(F32).reshape(lat * width, features)
    mid = wide + dot(o_ref[0], out_ref[...])
    mid_ref[:, 0] = mid.reshape(-1, mid_ref.shape[2], width, features).astype(BF16)


def full(shape):
    return pl.BlockSpec(shape, lambda *_: (0,) * len(shape), pipeline_mode=pl.Buffered(1))


def per_step(shape):
    return pl.BlockSpec((1,) + shape, lambda i: (i,) + (0,) * len(shape))


def cost(microseconds):
    return pl.CostEstimate(
        flops=microseconds * 10**9, bytes_accessed=4 << 20, transcendentals=2 * 10**6
    )


def grouped(peers, lat, width, features):
    return pl.BlockSpec((peers, 1, lat // peers, width, features), lambda i: (0, i, 0, 0, 0))


def spatial_forward(own, west, east, gain, qkv, out, peers):
    frames, lat, width, features = own.shape
    rows = lat * width
    blocks = lat // BH
    spans = sum(h - l for l, h in key_ranges(blocks, 3 * BH * width))
    groups = features // LANES
    outs = (
        ((3 * rows, features), BF16),
        ((rows, features), BF16),
        ((3 * rows, 2 * features), BF16),
        ((groups, spans, LANES), BF16),
        ((rows, features), BF16),
    )
    mid_shape = (peers, frames, lat // peers, width, features)
    return pl.pallas_call(
        spatial_forward_kernel,
        grid=(frames,),
        in_specs=[per_step((lat, width, features))] * 3
        + [full((1, features)), full(qkv.shape), full(out.shape)],
        out_specs=[per_step(shape) for shape, _ in outs] + [grouped(peers, lat, width, features)],
        out_shape=[pltpu.HBM((frames,) + shape, kind) for shape, kind in outs]
        + [pltpu.HBM(mid_shape, BF16)],
        compiler_params=pltpu.CompilerParams(vmem_limit_bytes=36 << 20),
        cost_estimate=cost(14),
        name="spatial_forward",
    )(*[from_hbm(a) for a in (own, west, east)], gain, from_hbm(qkv), from_hbm(out))


def temporal_kernel(
    mid_ref, cot_ref, gain_ref, qkv_ref, out_ref,
    both_ref, left_ref, right_ref,
    packed_ref, dproj_ref,
):
    peers, frames, lat, width, features = mid_ref.shape
    rows = peers * frames * width
    gain = gain_ref[...]
    scale = HDIM ** (-0.5)

    def by_row(ref, row):
        return ref[:, :, row].astype(F32).reshape(rows, features)

    for row in range(lat):
        part = slice(row * rows, (row + 1) * rows)
        unit, _ = normalized(by_row(mid_ref, row))
        left_ref[part, :features] = (unit * gain).astype(BF16)
        right_ref[part, 3 * features :] = by_row(cot_ref, row).astype(BF16)
    packed_ref[...] = dot(left_ref[:, :features], qkv_ref[...]).astype(BF16)
    dproj_ref[...] = dot(right_ref[:, 3 * features :], out_ref[...], 1, 1).astype(BF16)
    mask = head_mask(rows)
    key_col = lax.broadcasted_iota(jnp.int32, (rows, 4 * rows), 0) % width
    query_col = lax.broadcasted_iota(jnp.int32, (rows, 4 * rows), 1) % width
    same = key_col == query_col
    for row in range(lat):
        part = slice(row * rows, (row + 1) * rows)
        for g in range(features // LANES):
            lanes = [
                slice(s * features + g * LANES, s * features + (g + 1) * LANES) for s in range(3)
            ]
            queries = spread((packed_ref[part, lanes[0]] * scale).astype(BF16), mask)
            keys = packed_ref[part, lanes[1]]
            values = packed_ref[part, lanes[2]]
            scores = jnp.where(same, dot(keys, queries, 1, 1), -1e30)
            wide = softmax_rows(scores)
            weights = wide.astype(BF16)
            mixed = dot(weights, values, 0, 0)
            left_ref[part, lanes[1]] = gathered(mixed, rows).astype(BF16)
            d_out = spread(dproj_ref[part, lanes[0]], mask)
            d_weights = dot(values, d_out, 1, 1)
            delta = jnp.sum(wide * d_weights, axis=0, keepdims=True)
            d_scores = (wide * (d_weights - delta)).astype(BF16)
            d_query = gathered(dot(d_scores, keys, 0, 0), rows) * scale
            right_ref[part, lanes[0]] = d_query.astype(BF16)
            right_ref[part, lanes[1]] = dot(d_scores, queries).astype(BF16)
            right_ref[part, lanes[2]] = dot(weights, d_out).astype(BF16)
    layer = dot(left_ref[:, features:], out_ref[...])
    d_y = dot(right_ref[:, : 3 * features], qkv_ref[...], 1, 1)
    shape = (peers, frames, width, features)
    for row in range(lat):
        part = slice(row * rows, (row + 1) * rows)
        mid = by_row(mid_ref, row)
        unit, inverse = normalized(mid)
        d_mid = by_row(cot_ref, row) + norm_back(unit, inverse, gain, d_y[part])
        both_ref[:, :frames, row] = d_mid.reshape(shape).astype(BF16)
        both_ref[:, frames:, row] = (mid + layer[part]).reshape(shape).astype(BF16)


def temporal(mid, cot, gain, qkv, out):
    peers, frames, lat, width, features = mid.shape
    rows = peers * frames * lat * width
    return pl.pallas_call(
        temporal_kernel,
        out_shape=[
            pltpu.HBM((peers, 2 * frames, lat, width, features), BF16),
            pltpu.HBM((rows, 2 * features), BF16),
            pltpu.HBM((rows, 4 * features), BF16),
        ],
        scratch_shapes=[
            pltpu.VMEM((rows, 3 * features), BF16),
            pltpu.VMEM((rows, features), BF16),
        ],
        compiler_params=pltpu.CompilerParams(vmem_limit_bytes=56 << 20),
        cost_estimate=cost(18),
        name="temporal",
    )(mid, cot, gain, qkv, out)


def back_projection_kernel(dmid_ref, out_ref, dproj_ref):
    rows, features = dproj_ref.shape[1:]
    dmid = dmid_ref[...].astype(F32).reshape(rows, features).astype(BF16)
    dproj_ref[0] = dot(dmid, out_ref[...], 1, 1).astype(BF16)


def back_projection(dmid, out, frames):
    peers, _, each, width, features = dmid.shape
    rows = peers * each * width
    return pl.pallas_call(
        back_projection_kernel,
        grid=(frames,),
        in_specs=[grouped(peers, peers * each, width, features), full(out.shape)],
        out_specs=per_step((rows, features)),
        out_shape=pltpu.HBM((frames, rows, features), BF16),
        compiler_params=pltpu.CompilerParams(vmem_limit_bytes=12 << 20),
        cost_estimate=cost(30),
        name="back_projection",
    )(dmid, out)


def spatial_backward_kernel(
    dproj_ref, qkv_ref, q_ref, kv_ref, p_ref,
    dq_ref, dkv_ref, own_ref, west_ref, east_ref,
    acc_ref,
):
    _, lat, width, features = own_ref.shape
    rows = BH * width
    blocks = lat // BH
    step = 3 * rows
    mask = head_mask(rows)
    acc_ref[...] = jnp.zeros_like(acc_ref)
    offset = 0
    for b, (low, high) in enumerate(key_ranges(blocks, step)):
        span = high - low
        block = slice(b * rows, (b + 1) * rows)
        for g in range(features // LANES):
            lanes = slice(g * LANES, (g + 1) * LANES)
            late = slice(features + g * LANES, features + (g + 1) * LANES)
            queries = spread(q_ref[0, block, lanes], mask)
            d_out = spread(dproj_ref[0, block, lanes], mask)
            keys = kv_ref[0, low:high, lanes]
            values = kv_ref[0, low:high, late]
            weights = p_ref[0, g, offset : offset + span]
            wide = weights.astype(F32)
            d_weights = dot(values, d_out, 1, 1)
            delta = jnp.sum(wide * d_weights, axis=0, keepdims=True)
            d_scores = (wide * (d_weights - delta)).astype(BF16)
            d_query = gathered(dot(d_scores, keys, 0, 0), rows) * HDIM ** (-0.5)
            dq_ref[0, block, lanes] = d_query.astype(BF16)
            acc_ref[low:high, lanes] += dot(d_scores, queries)
            acc_ref[low:high, late] += dot(weights, d_out)
        offset += span
    dkv_ref[0] = acc_ref[...].astype(BF16)
    for b in range(blocks):
        part = slice(b * step, (b + 1) * step)
        d_y = dot(dkv_ref[0, part], qkv_ref[:, features:], 1, 1)
        block = slice(b * rows, (b + 1) * rows)
        d_own = d_y[rows : 2 * rows] + dot(dq_ref[0, block], qkv_ref[:, :features], 1, 1)
        for ref, value in ((west_ref, d_y[:rows]), (own_ref, d_own), (east_ref, d_y[2 * rows :])):
            ref[0, b * BH : (b + 1) * BH] = value.reshape(BH, width, features).astype(BF16)


def spatial_backward(dproj, qkv, q, kv, p, lat):
    frames, rows, features = dproj.shape
    width = rows // lat
    outs = (
        (rows, features),
        (3 * rows, 2 * features),
        (lat, width, features),
        (lat, width, features),
        (lat, width, features),
    )
    return pl.pallas_call(
        spatial_backward_kernel,
        grid=(frames,),
        in_specs=[
            per_step((rows, features)),
            full(qkv.shape),
            per_step(q.shape[1:]),
            per_step(kv.shape[1:]),
            per_step(p.shape[1:]),
        ],
        out_specs=[per_step(shape) for shape in outs],
        out_shape=[
            (pltpu.HBM if at >= 2 else jax.ShapeDtypeStruct)((frames,) + shape, BF16)
            for at, shape in enumerate(outs)
        ],
        scratch_shapes=[
            pltpu.VMEM((3 * rows, 2 * features), F32),
        ],
        compiler_params=pltpu.CompilerParams(vmem_limit_bytes=36 << 20),
        cost_estimate=cost(20),
        name="spatial_backward",
    )(*[from_hbm(a) for a in (dproj, qkv, q, kv, p)])


def final_kernel(tokens_ref, gain_ref, dmid_ref, own_ref, first_ref, second_ref, grad_ref):
    _, lat, width, features = tokens_ref.shape

    def flat(ref):
        return ref[0].astype(F32).reshape(lat * width, features)

    unit, inverse = normalized(flat(tokens_ref))
    d_y = flat(own_ref) + flat(first_ref) + flat(second_ref)
    d_mid = dmid_ref[...].astype(F32).reshape(lat * width, features)
    grad = d_mid + norm_back(unit, inverse, gain_ref[...], d_y)
    grad_ref[0] = grad.reshape(lat, width, features)


def final_norm(tokens, gain, dmid, own, first, second):
    frames, lat, width, features = tokens.shape
    block = per_step((lat, width, features))
    return pl.pallas_call(
        final_kernel,
        grid=(frames,),
        in_specs=[block, full((1, features)), grouped(dmid.shape[0], lat, width, features)]
        + [block] * 3,
        out_specs=block,
        out_shape=jax.ShapeDtypeStruct(tokens.shape, F32),
        compiler_params=pltpu.CompilerParams(vmem_limit_bytes=16 << 20),
        cost_estimate=cost(3),
        name="final_norm",
    )(tokens, gain, dmid, own, first, second)


def split_store(core_ref, term, keep_ref, send_ref):
    tiles, rows, columns = keep_ref.shape
    pairs = term.reshape(tiles, 2, rows, columns)
    first = core_ref[0] == 0
    for tile in range(tiles):
        even, odd = pairs[tile, 0], pairs[tile, 1]
        keep_ref[tile] = jnp.where(first, even, odd).astype(BF16)
        send_ref[tile] = jnp.where(first, odd, even).astype(BF16)


def term_time_kernel(core_ref, left_ref, right_ref, keep_ref, send_ref):
    split_store(core_ref, dot(left_ref[...], right_ref[...], 0, 0), keep_ref, send_ref)


def split_call(kernel, core, operands, specs, features, tiles, name, flops):
    shape = (tiles, features // (2 * tiles), 4 * features)
    block = pl.BlockSpec(shape[:2] + (features,), lambda i, core: (0, 0, i))
    return pl.pallas_call(
        kernel,
        grid_spec=pltpu.PrefetchScalarGridSpec(
            num_scalar_prefetch=1, grid=(4,), in_specs=specs, out_specs=[block, block]
        ),
        out_shape=[pltpu.HBM(shape, BF16)] * 2,
        compiler_params=pltpu.CompilerParams(vmem_limit_bytes=24 << 20),
        cost_estimate=pl.CostEstimate(flops=flops, bytes_accessed=1, transcendentals=0),
        name=name,
    )(core, *operands)


def term_time(core, left, right, tiles):
    rows, double = left.shape
    features = double // 2
    specs = [
        pl.BlockSpec((rows, features), lambda i, core: (0, i // 3)),
        pl.BlockSpec((rows, features), lambda i, core: (0, i)),
    ]
    return split_call(
        term_time_kernel, core, (from_hbm(left), from_hbm(right)), specs, features, tiles,
        "term_time", 1,
    )


def term_space_kernel(core_ref, y_ref, dq_ref, dkv_ref, o_ref, dmid_ref, keep_ref, send_ref):
    step = pl.program_id(0)
    frames, ext, features = y_ref.shape
    own = dq_ref.shape[1]

    @pl.when(step == 0)
    def _():
        part = BH * dmid_ref.shape[3]
        blocks = own // part
        pieces = [
            y_ref[f, (3 * b + 1) * part : (3 * b + 2) * part]
            for f in range(frames)
            for b in range(blocks)
        ]
        left = jnp.concatenate(pieces, axis=0)
        right = dq_ref[...].reshape(frames * own, features)
        split_store(core_ref, dot(left, right, 0, 0), keep_ref, send_ref)

    @pl.when((step == 1) | (step == 2))
    def _():
        left = y_ref[...].reshape(frames * ext, features)
        right = dkv_ref[...].reshape(frames * ext, features)
        split_store(core_ref, dot(left, right, 0, 0), keep_ref, send_ref)

    @pl.when(step == 3)
    def _():
        left = o_ref[...].reshape(frames * own, features)
        right = [dmid_ref[:, f].astype(F32).reshape(own, features) for f in range(frames)]
        right = jnp.concatenate(right, axis=0).astype(BF16)
        split_store(core_ref, dot(left, right, 0, 0), keep_ref, send_ref)


def term_space(core, y, dq, dkv, o, dmid, tiles):
    features = y.shape[-1]

    def whole(array):
        return pl.BlockSpec(
            array.shape, lambda i, core: (0,) * array.ndim, pipeline_mode=pl.Buffered(1)
        )

    specs = [
        whole(y),
        whole(dq),
        pl.BlockSpec(dkv.shape[:2] + (features,), lambda i, core: (0, 0, jnp.clip(i - 1, 0, 1))),
        whole(o),
        pl.BlockSpec(
            (dmid.shape[0], y.shape[0]) + dmid.shape[2:],
            lambda i, core: (0,) * dmid.ndim,
            pipeline_mode=pl.Buffered(1),
        ),
    ]
    return split_call(
        term_space_kernel, core, (y, dq, dkv, o, dmid), specs, features, tiles, "term_space", 1,
    )


def fold(total, row_ref, base, peers, put):
    rows, columns = total.shape
    across = columns // 128
    each = rows // peers
    for c in range(across):
        at = base + c * rows
        row_ref[at : at + rows] = total[:, c * 128 : (c + 1) * 128]
    for peer in range(peers):
        for r in range(0, each, 2):
            start = base + peer * each + r
            pair = [row_ref[pl.ds(start + k, across, stride=rows)] for k in range(2)]
            put(peer, slice(r * across, (r + 2) * across), jnp.concatenate(pair, axis=0).astype(BF16))


def pair_fold_kernel(peers, keep_ref, got_ref, sum_ref, row_ref):
    tiles, rows, columns = keep_ref.shape
    for tile in range(tiles):

        def put(peer, at, value):
            sum_ref[tile * peers + peer, at] = value

        total = keep_ref[tile].astype(F32) + got_ref[tile].astype(F32)
        fold(total, row_ref, tile * rows * columns // 128, peers, put)


def exchanged_pair(send):
    return lax.ppermute(send, "core", [(0, 1), (1, 0)])


def paired(keep, send, peers):
    got = exchanged_pair(send)
    tiles, rows, columns = keep.shape
    at_once = tiles // 4
    height = rows // peers * columns // 128
    block = pl.BlockSpec((at_once, rows, columns), lambda i: (i, 0, 0))
    return pl.pallas_call(
        functools.partial(pair_fold_kernel, peers),
        grid=(4,),
        in_specs=[block, block],
        out_specs=pl.BlockSpec((at_once * peers, height, 128), lambda i: (i, 0, 0)),
        out_shape=jax.ShapeDtypeStruct((tiles * peers, height, 128), BF16),
        scratch_shapes=[pltpu.VMEM((at_once * columns // 128 * rows, 128), F32)],
        compiler_params=pltpu.CompilerParams(vmem_limit_bytes=16 << 20),
        cost_estimate=pl.CostEstimate(flops=1, bytes_accessed=1, transcendentals=0),
        name="pair_fold",
    )(from_hbm(keep), got)


def sum_fold_kernel(arrived_ref, sum_ref, row_ref):
    def put(peer, at, value):
        sum_ref[peer, at] = value

    total = jnp.sum(arrived_ref[...].astype(F32), axis=0)
    fold(total, row_ref, 0, sum_ref.shape[0], put)


def sum_fold(arrived, peers):
    _, rows, columns = arrived.shape
    return pl.pallas_call(
        sum_fold_kernel,
        out_shape=pltpu.HBM((peers, rows // peers * columns // 128, 128), BF16),
        scratch_shapes=[pltpu.VMEM((columns // 128 * rows, 128), F32)],
        compiler_params=pltpu.CompilerParams(vmem_limit_bytes=16 << 20),
        cost_estimate=pl.CostEstimate(flops=1, bytes_accessed=1, transcendentals=0),
        name="sum_fold",
    )(arrived)


def ring_sum(chunks, axis):
    size = lax.axis_size(axis)
    me = lax.axis_index(axis).astype(jnp.uint32)

    def chunk(by):
        at = lax.bitwise_and(me + jnp.uint32(by), jnp.uint32(size - 1))
        return lax.dynamic_index_in_dim(chunks, at, 0, keepdims=False)

    total = chunk(0).astype(F32)
    for by in range(1, size):
        moved = lax.ppermute(chunk(by), axis, [(i, (i + by) % size) for i in range(size)])
        total = total + moved.astype(F32)
    return total


def summed_over_xhi(chunks):
    z, xhi = lax.axis_size("z"), lax.axis_size("xhi")
    split = chunks.reshape((z, xhi) + chunks.shape[1:])
    return ring_sum(jnp.swapaxes(split, 0, 1), "xhi").astype(BF16)


def spread_out(mine):
    return lax.all_to_all(mine, ("xlo", "y", "z", "xhi"), 0, 0, tiled=False)


def shifted(shard, by):
    size = lax.axis_size(TILE)
    return lax.ppermute(shard, TILE, [(i, (i + by) % size) for i in range(size)])


def from_hbm(array):
    return pltpu.with_memory_space_constraint(array, pltpu.HBM)


def own_rows(weight):
    count = lax.axis_size(TILE + FRAME)
    per_device = weight.shape[0] // count
    at = lax.axis_index(TILE + FRAME) * per_device
    return lax.dynamic_slice_in_dim(weight, at, per_device, axis=0).astype(F32)


def finish_kernel(scale, arrived_ref, weight_ref, gain_ref, d_gain_ref, d_qkv_ref, d_out_ref):
    rows, wide = d_qkv_ref.shape
    total = jnp.sum(arrived_ref[...].astype(F32), axis=0) * scale
    across = total.shape[0] // rows
    own = wide // 128
    for r in range(rows):
        for c in range(across):
            part = total[r * across + c : r * across + c + 1]
            if c < own:
                d_qkv_ref[r : r + 1, c * 128 : (c + 1) * 128] = part
            else:
                d_out_ref[r : r + 1, (c - own) * 128 : (c - own + 1) * 128] = part
    along = jnp.sum(weight_ref[...] * d_qkv_ref[...], axis=1, keepdims=True)
    d_gain_ref[...] = along / gain_ref[...]


def finished(arrived, weight, gain, tokens):
    rows, wide = weight.shape
    features = arrived.shape[1] * 128 // rows - wide
    d_gain, d_qkv, d_out = pl.pallas_call(
        functools.partial(finish_kernel, 1.0 / math.sqrt(tokens)),
        out_shape=[
            jax.ShapeDtypeStruct((rows, 1), F32),
            jax.ShapeDtypeStruct((rows, wide), F32),
            jax.ShapeDtypeStruct((rows, features), F32),
        ],
        compiler_params=pltpu.CompilerParams(vmem_limit_bytes=12 << 20),
        cost_estimate=cost(2),
        name="finish",
    )(arrived, weight, gain.reshape(rows, 1))
    return d_gain.reshape(rows), d_qkv, d_out


def shards(tokens, gain_space, qkv_space, out_space, gain_time, qkv_time, out_time, cotangent):
    frames, lat, width, features = tokens.shape
    total = frames * lat * width * lax.axis_size(TILE) * lax.axis_size(FRAME)
    gain_s = gain_space.reshape(1, features)
    gain_t = gain_time.reshape(1, features)
    core = lax.axis_index("core").astype(jnp.int32).reshape(1)
    tiles = lax.axis_size(("xlo", "y"))

    peers = lax.axis_size(FRAME)

    def exchanged(chunks):
        return lax.all_to_all(chunks, FRAME, 0, 0, tiled=False)

    west = shifted(tokens, 1)
    east = shifted(tokens, -1)
    cot_chunks = cotangent.reshape(frames, peers, lat // peers, width, features)
    cot_rows = exchanged(cot_chunks.transpose(1, 0, 2, 3, 4))
    y_s, q_s, kv_s, p_s, o_s, mid = spatial_forward(
        tokens, west, east, gain_s, qkv_space, out_space, peers
    )
    slices = [own_rows(a) for a in (qkv_space, gain_space, qkv_time, gain_time)]
    mid, cot_rows = lax.optimization_barrier((mid, cot_rows))
    mid_rows, slices = lax.optimization_barrier((exchanged(mid), slices))
    both_rows, left_t, right_t = temporal(mid_rows, cot_rows, gain_t, qkv_time, out_time)
    both = exchanged(both_rows)
    keep_t, send_t = term_time(core, left_t, right_t, tiles)
    mine_t = (keep_t.astype(F32) + exchanged_pair(send_t).astype(F32)).astype(BF16)
    dproj = back_projection(both, out_space, frames)
    dproj, mine_t = lax.optimization_barrier((dproj, mine_t))
    arrived_t = lax.all_to_all(mine_t, ("xlo", "y"), 0, 0, tiled=False)
    dq, dkv, own, for_west, for_east = spatial_backward(dproj, qkv_space, q_s, kv_s, p_s, lat)
    from_east = shifted(for_west, -1)
    from_west = shifted(for_east, 1)
    keep_s, send_s = term_space(core, y_s, dq, dkv, o_s, both, tiles)
    folded_t = sum_fold(arrived_t, peers)
    send_s, folded_t = lax.optimization_barrier((send_s, folded_t))
    mine_s = paired(keep_s, send_s, peers)
    after_x = summed_over_xhi(folded_t)
    mine_s, after_x = lax.optimization_barrier((mine_s, after_x))
    arrived_s = spread_out(mine_s)
    summed_t = ring_sum(after_x, "z")[None]
    layer_out = both[:, frames:].transpose(1, 0, 2, 3, 4).reshape(tokens.shape)
    grad_tokens = final_norm(tokens, gain_s, both, own, from_east, from_west)
    return (
        (layer_out, grad_tokens)
        + finished(arrived_s, slices[0], slices[1], total)
        + finished(summed_t, slices[2], slices[3], total)
    )


def solution(mesh):
    fine = Mesh(mesh.devices.reshape(2, 4, 2, 4, 2), TILE + FRAME)
    token_spec = P(FRAME, None, TILE, None)
    row_spec = P(TILE + FRAME)
    return jax.shard_map(
        shards,
        mesh=fine,
        in_specs=(token_spec, P(), P(), P(), P(), P(), P(), token_spec),
        out_specs=(token_spec, token_spec) + (row_spec,) * 6,
        check_vma=False,
    )
```
